32 devices in a mesh: grp: 2 (over x), loc: 16 (over z, y, core).
Axes of the slice: x: 2, y: 2, z: 4, core: 2. Of those that a mesh axis runs over, the one named last changes fastest.
Arguments:
- latents: bfloat16 [16384, 2048], P(('grp', 'loc')), parts along dimension 0, may hold values from -6 to 6
- obs_inst: int32 [16384, 1], P(('grp', 'loc')), parts along dimension 0, may hold values from 0 to 15; in each aligned block of 512 rows (0 to 511, 512 to 1023, ...) at most 64 rows name the same one
- owner_slot: int32 [16], replicated, may hold values from 0 to 15, each once
- head_weights: bfloat16 [16, 2048, 512], P('loc'), may hold values from -0.125 to 0.125
- error_weight: float32 [16, 512], P('loc'), may hold values from 0.25 to 4
- block_pattern: int32 [16, 16, 4], P('loc'), may hold values 0 or 1
- targets: bfloat16 [16384, 512], P(('grp', 'loc')), parts along dimension 0, may hold values from -6 to 6
Outputs:
- latent_grad: bfloat16 [16384, 2048], P(('grp', 'loc')), parts along dimension 0
- head_grad: float32 [32, 2048, 512], P(('grp', 'loc')), parts along dimension 0
The draws below stay inside these ranges and needn't reach their ends.
There are 2 independent parts, one for each index of `grp`. The reference program is written for one: setup_inputs(seed, part) draws one part's arguments, and reference() takes and returns one part's arrays. A program takes and returns all parts, laid end to end along the dimension named above; an argument that names none is the same for every part. Nothing has to cross between parts.
Inputs may be any that keep to these rules, and one draw needn't show every extreme that they name: `obs_inst`: in each aligned block of 512 rows (the rows of one device) no instrument is named by more than 64 rows; some instrument is named by exactly 64 rows in some blocks. `owner_slot`: each row number appears once.
All inputs are finite; a program needn't handle non-finite values. No bound on the sum of `block_pattern` on one device may be relied on, other than what follows from the above.
Results may differ from the reference program's by a relative error of at most 0.0048.
Values may be sent and summed in bfloat16 or wider, within the bound.
No kernel may reach another device: no remote copies, remote signals or barrier semaphores. Data moves between devices by JAX's collectives and lax.ppermute only.
A program may use at most 64 MiB of HBM per device.

```python
import math
import jax
import jax.numpy as jnp
import numpy as np
from jax import lax

D = 2048
CH = 512
BLK = 128
INST = 16
OBS_DEV = 512
OBS = 8192
CAP = 64
N_LOC = 16


def plant(array, own_key, least, top_value):
    extent = array.shape
    place = [jax.random.randint(jax.random.fold_in(own_key, axis), (), 0, extent[axis]) for axis in range(len(extent))]
    array = array.at[tuple(place)].set(least)
    longest = extent.index(max(extent))
    place[longest] = (place[longest] + 1) % extent[longest]
    return array.at[tuple(place)].set(top_value)


def levels(rng, extent, pieces, smallest, largest):
    level = 1.0
    for position, blocks in pieces:
        draws = jax.random.uniform(jax.random.fold_in(jax.random.fold_in(rng, 6), position), (blocks,), jnp.float32, smallest / len(pieces), largest / len(pieces))
        level = level * jnp.repeat(jnp.exp(draws), extent[position] // blocks).reshape((-1,) + (1,) * (len(extent) - 1 - position))
    return level


def assign_block(own_key, own, number, rows, amount, top, most, lean):
    ranking = jax.random.permutation(own_key, amount)
    heavy_load, usual = shares(amount, rows * top, most, lean, True), shares(amount, rows * top, most, lean, False)
    places = jnp.arange(amount)

    def named(sizes, offset_by):
        used = int((sizes > 0).sum())
        fixed = max(1, used // 4)
        shifted = fixed + (places - fixed + offset_by * (used - fixed)) % max(1, amount - fixed)
        return jnp.zeros((amount,), jnp.int32).at[ranking[jnp.where(places < fixed, places, shifted)]].set(jnp.asarray(sizes, jnp.int32))

    sizes = jnp.where(number % 4 == 0, named(heavy_load, number // 4), named(usual, number - number // 4 - 1))
    mixed = jax.random.permutation(jax.random.fold_in(own, 3), amount)
    donor, sink = mixed[0:amount // 2 * 2:2], mixed[1:amount // 2 * 2:2]
    room = jnp.minimum(sizes[donor] - 1, most - sizes[sink]) // 2
    room = jnp.where((donor == ranking[0]) | (sink == ranking[0]) | (sizes[sink] == 0), 0, jnp.maximum(room, 0))
    shifted = jax.random.randint(jax.random.fold_in(own, 4), (amount // 2,), 0, 1 << 20) % (room + 1)
    sizes = sizes.at[donor].add(-shifted).at[sink].add(shifted)
    items = jnp.searchsorted(jnp.cumsum(sizes), jnp.arange(rows * top), side="right").astype(jnp.int32)
    grid = items.reshape(top, rows).T
    grid = grid[jax.random.permutation(jax.random.fold_in(own, 1), rows)]
    offset_by = jax.random.randint(jax.random.fold_in(own, 2), (rows, 1), 0, top)
    return jnp.take_along_axis(grid, (jnp.arange(top)[None, :] + offset_by) % top, axis=1)


def shares(number_of, total, reach, skew, full):
    weights = [(1 << 20) // math.isqrt(standing ** skew) + 1 for standing in range(1, number_of + 1)]
    largest = reach if full else min(reach, max(-(-total // number_of), total * weights[0] // sum(weights)))
    least = 1 if total - largest >= number_of - 1 else 0
    holding, spare = [largest] + [least] * (number_of - 1), total - largest - least * (number_of - 1)
    while spare > 0:
        free = [i for i in range(1, number_of) if holding[i] < largest] or [i for i in range(1, number_of) if holding[i] < reach]
        whole, budget = sum([weights[i] for i in free]), spare
        for i in free:
            more = min(reach - holding[i], max(1, budget * weights[i] // whole), spare)
            holding[i] = holding[i] + more
            spare = spare - more
    return np.array(holding)


def centred(own_key, shape, width, most, shards=(), kind=jnp.bfloat16):
    factor_of = levels(own_key, shape, shards, -0.22, 0.18) if shards else 1.0
    array = jax.random.normal(own_key, shape, jnp.float32) * width * factor_of
    return jnp.minimum(jnp.maximum(array, -most), most).astype(kind)


def setup_inputs(seed: int = 0, part: int = 0) -> dict:
    splits = jax.random.split(jax.random.key(seed), 8)
    part_keys = jax.random.split(jax.random.fold_in(splits[7], part), 8)
    latents = centred(part_keys[0], (OBS, D), 1.0, 6.0, ((0, 16),))
    obs_inst_keys = jax.random.split(jax.random.fold_in(part_keys[1], 1), OBS // OBS_DEV)
    obs_inst_turns = jax.random.permutation(jax.random.fold_in(part_keys[1], 3), OBS // OBS_DEV)
    obs_inst = jax.vmap(lambda own, number: assign_block(jax.random.fold_in(part_keys[1], 2), own, number, OBS_DEV, INST, 1, CAP, 2))(obs_inst_keys, obs_inst_turns).reshape((OBS, 1))
    owner_slot = jax.random.permutation(splits[2], INST).astype(jnp.int32)
    head_weights = centred(splits[3], (INST, D, CH), D ** -0.5, 0.125, ((0, 16),))
    error_weight = jnp.clip(jnp.exp(math.log(4.0) - 2.7725887 * jax.random.uniform(splits[4], (INST, CH), jnp.float32) ** levels(splits[4], (INST, CH), ((0, 16),), -0.2, 0.2)), 0.25, 4.0)
    block_pattern = plant((jax.random.randint(splits[5], (INST, D // BLK, CH // BLK), 0, 4) < 3).astype(jnp.int32), jax.random.fold_in(splits[5], 1), 0, 1)
    targets = centred(part_keys[6], (OBS, CH), 1.0, 6.0, ((0, 16),))
    return {"latents": latents, "obs_inst": obs_inst, "owner_slot": owner_slot, "head_weights": head_weights, "error_weight": error_weight, "block_pattern": block_pattern, "targets": targets}


def reference(latents, obs_inst, owner_slot, head_weights, error_weight, block_pattern, targets):
    slot_of = owner_slot[obs_inst[:, 0]]
    slot_rows = N_LOC * CAP
    block_mask = jnp.repeat(jnp.repeat(block_pattern, BLK, 1), BLK, 2)
    padded_latents = jnp.concatenate([latents, jnp.zeros((1, D), latents.dtype)], 0)
    padded_targets = jnp.concatenate([targets, jnp.zeros((1, CH), targets.dtype)], 0)

    def per_slot(number):
        picked = jnp.nonzero(slot_of == number, size=slot_rows, fill_value=OBS)[0].astype(jnp.int32)
        rows_in = padded_latents[picked]
        wanted = padded_targets[picked]
        effective = head_weights[number] * block_mask[number].astype(head_weights.dtype)
        predicted = jnp.dot(rows_in, effective, preferred_element_type=jnp.float32)
        residual = (error_weight[number][None, :] * (predicted - wanted.astype(jnp.float32))).astype(jnp.bfloat16)
        raw_grad = jnp.dot(rows_in.T, residual, preferred_element_type=jnp.float32) * block_mask[number].astype(jnp.float32)
        row_grad = jnp.dot(residual, effective.T, preferred_element_type=jnp.float32).astype(jnp.bfloat16)
        return (raw_grad, row_grad, picked)
    raw_grad, row_grad, picked = lax.map(per_slot, jnp.arange(INST, dtype=jnp.int32))
    squares = jnp.sum(raw_grad * raw_grad)
    factor = jnp.minimum(1.0, math.sqrt(INST * D * CH) / jnp.sqrt(squares + 1e-06))
    head_grad = raw_grad * factor
    latent_grad = jnp.zeros((OBS + 1, D), jnp.bfloat16).at[picked.reshape(-1)].set(row_grad.reshape(-1, D).astype(jnp.bfloat16))[:OBS]
    return (latent_grad, head_grad)
```

```python
import math

import jax
import jax.numpy as jnp
from jax import lax
from jax.sharding import PartitionSpec as P

BLK = 128


def per_device(latents, obs_inst, owner_slot, head_weights, error_weight, block_pattern, targets):
    members = lax.axis_size("loc")
    local_heads, width, channels = head_weights.shape
    instruments = local_heads * members
    rows_dev = latents.shape[0]
    capacity = 2 * rows_dev // instruments
    numbers = jnp.arange(instruments, dtype=jnp.int32)
    inst_hit = obs_inst == numbers[None, :]
    slot_of = jnp.sum(jnp.where(inst_hit, owner_slot[None, :], 0), 1)
    slot_hit = (slot_of[:, None] == numbers[None, :]).astype(jnp.int32)
    rank_in = jnp.sum((jnp.cumsum(slot_hit, 0) - 1) * slot_hit, 1)
    placed = slot_of * capacity + rank_in
    send_rows = jnp.zeros((instruments * capacity, width), latents.dtype).at[placed].set(latents)
    send_targets = (
        jnp.zeros((instruments * capacity, channels), targets.dtype).at[placed].set(targets)
    )
    block_mask = jnp.repeat(jnp.repeat(block_pattern, BLK, 1), BLK, 2)
    effective = head_weights * block_mask.astype(head_weights.dtype)
    got = lax.all_to_all(
        jnp.concatenate([send_rows, send_targets], 1), "loc", split_axis=0, concat_axis=0, tiled=True
    )
    arrived = got[:, :width]
    predicted = jnp.dot(arrived, effective[0], preferred_element_type=jnp.float32)
    misfit = predicted - got[:, width:].astype(jnp.float32)
    residual = (error_weight * misfit).astype(jnp.bfloat16)
    row_grad = lax.dot_general(
        residual, effective[0], (((1,), (1,)), ((), ())), preferred_element_type=jnp.float32
    ).astype(jnp.bfloat16)
    returned = lax.all_to_all(row_grad, "loc", split_axis=0, concat_axis=0, tiled=True)
    raw_grad = lax.dot_general(
        arrived, residual, (((0,), (0,)), ((), ())), preferred_element_type=jnp.float32
    ) * block_mask[0].astype(jnp.float32)
    squares = jnp.broadcast_to(jnp.sum(raw_grad * raw_grad), (8, 128))
    step = 1
    while step < members:
        squares = squares + lax.ppermute(squares, "loc", [(i, i ^ step) for i in range(members)])
        step *= 2
    squares = squares[0, 0]
    factor = jnp.minimum(1.0, math.sqrt(instruments * width * channels) / jnp.sqrt(squares + 1e-06))
    head_grad = (raw_grad * factor)[None]
    latent_grad = returned[placed]
    return (latent_grad, head_grad)


def solution(mesh):
    in_specs = (
        P(("grp", "loc"), None),
        P(("grp", "loc"), None),
        P(),
        P("loc", None, None),
        P("loc", None),
        P("loc", None, None),
        P(("grp", "loc"), None),
    )
    out_specs = (P(("grp", "loc"), None), P(("grp", "loc"), None, None))
    return jax.shard_map(
        per_device, mesh=mesh, in_specs=in_specs, out_specs=out_specs, check_vma=False
    )
```

```python
import functools
import math

import jax
import jax.numpy as jnp
from jax import lax
from jax.experimental import pallas as pl
from jax.experimental.pallas import tpu as pltpu
from jax.sharding import PartitionSpec as P

BLK = 128
F32 = jnp.float32
BF16 = jnp.bfloat16
VMEM = pl.BlockSpec(memory_space=pltpu.VMEM)
SMEM = pl.BlockSpec(memory_space=pltpu.SMEM)
PARAMS = pltpu.CompilerParams(vmem_limit_bytes=48 * 1024 * 1024)


def dot(a, b, ca=1, cb=0):
    return lax.dot_general(a, b, (((ca,), (cb,)), ((), ())), preferred_element_type=F32)


def cost(flops, nbytes):
    return pl.CostEstimate(flops=int(flops), bytes_accessed=int(nbytes), transcendentals=0)


def places(inst, owner_ref, heads):
    rows = inst.shape[1]
    slot = jnp.zeros_like(inst)
    for k in range(heads):
        slot = jnp.where(inst == k, owner_ref[k], slot)
    hit = lax.broadcasted_iota(jnp.int32, (heads, rows), 0) == slot
    upto = lax.broadcasted_iota(jnp.int32, (rows, rows), 0) <= lax.broadcasted_iota(
        jnp.int32, (rows, rows), 1
    )
    count = dot(hit.astype(BF16), upto.astype(BF16))
    rank = jnp.sum(jnp.where(hit, count, 0.0), 0, keepdims=True).astype(jnp.int32) - 1
    return slot, rank


def one_hot_rows(pos, start, size):
    number = lax.broadcasted_iota(jnp.int32, (size, pos.shape[1]), 0) + start
    return (number == pos).astype(F32).astype(BF16)


def one_hot_back(pos, size):
    column = jnp.transpose(jnp.broadcast_to(pos.astype(F32), (128, pos.shape[1])))[:, :1]
    number = lax.broadcasted_iota(jnp.int32, (pos.shape[1], size), 1)
    return (number == column.astype(jnp.int32)).astype(F32).astype(BF16)


def prep_kernel(heads, capacity, inst_ref, owner_ref, x_ref, t_ref, out_ref, place_ref):
    size, width = out_ref.shape[0], x_ref.shape[1]
    step = pl.program_id(0)

    @pl.when(step == 0)
    def _():
        slot, rank = places(inst_ref[...], owner_ref, heads)
        place_ref[...] = jnp.broadcast_to(slot * capacity + rank, place_ref.shape)

    pick = one_hot_rows(place_ref[0:1, :], step * size, size)
    out_ref[:, :width] = dot(pick, x_ref[...]).astype(BF16)
    out_ref[:, width:] = dot(pick, t_ref[...]).astype(BF16)


def back_kernel(heads, capacity, inst_ref, owner_ref, back_ref):
    slot, rank = places(inst_ref[...], owner_ref, heads)
    back_ref[...] = one_hot_back(slot * capacity + rank, back_ref.shape[1])


def effective_kernel(w_ref, mask_ref, out_ref):
    for block in range(mask_ref.shape[0]):
        here = slice(block * BLK, (block + 1) * BLK)
        out_ref[here, :] = (w_ref[here, :].astype(F32) * mask_ref[block : block + 1, :]).astype(BF16)


def head_kernel(width, x_ref, eff_ref, weight_ref, grad_ref, res_ref):
    predicted = dot(x_ref[:, :width], eff_ref[...])
    residual = (weight_ref[...] * (predicted - x_ref[:, width:].astype(F32))).astype(BF16)
    res_ref[...] = residual
    grad_ref[...] = dot(residual, eff_ref[...], 1, 1).astype(BF16)


def raw_kernel(x_ref, res_ref, mask_ref, raw_ref, square_ref):
    step = pl.program_id(0)
    size, channels = raw_ref.shape
    raw = dot(x_ref[...], res_ref[...], 0, 0)

    @pl.when(step == 0)
    def _():
        square_ref[...] = jnp.zeros_like(square_ref)

    for block in range(size // BLK):
        here = slice(block * BLK, (block + 1) * BLK)
        part = raw[here, :] * mask_ref[pl.ds(step * (size // BLK) + block, 1), :]
        raw_ref[here, :] = part
        total = jnp.sum((part * part).reshape(BLK // 8, 8, channels), 0)
        for lane in range(channels // 128):
            square_ref[...] += total[:, lane * 128 : (lane + 1) * 128]


def scale_kernel(limit, raw_ref, square_ref, out_ref):
    squares = jnp.sum(square_ref[...], keepdims=True)
    factor = jnp.minimum(1.0, limit / jnp.sqrt(squares + 1e-06))
    out_ref[...] = (raw_ref[...] * factor)[None]


def place_back_kernel(back_ref, got_ref, out_ref):
    out_ref[...] = dot(back_ref[...], got_ref[...]).astype(BF16)


def per_device(latents, obs_inst, owner_slot, head_weights, error_weight, block_pattern, targets):
    members = lax.axis_size("loc")
    local_heads, width, channels = head_weights.shape
    heads = local_heads * members
    rows = latents.shape[0]
    capacity = 2 * rows // heads
    padded = heads * capacity
    wide = width + channels
    inst = obs_inst.reshape(1, rows)
    mask = jnp.repeat(block_pattern[0], BLK, 1).astype(F32)

    def whole(shape):
        return pl.BlockSpec(shape, lambda i: (0, 0))

    cut = 4
    send = pl.pallas_call(
        functools.partial(prep_kernel, heads, capacity),
        grid=(cut,),
        in_specs=[whole((1, rows)), SMEM, whole((rows, width)), whole((rows, channels))],
        out_specs=pl.BlockSpec((padded // cut, wide), lambda i: (i, 0)),
        out_shape=jax.ShapeDtypeStruct((padded, wide), BF16),
        scratch_shapes=[pltpu.VMEM((8, rows), jnp.int32)],
        compiler_params=PARAMS,
        cost_estimate=cost(2 * padded * rows * wide, 2 * (padded + rows) * wide),
        name="prep",
    )(inst, owner_slot, latents, targets)
    got = lax.all_to_all(send, "loc", split_axis=0, concat_axis=0, tiled=True)

    back = pl.pallas_call(
        functools.partial(back_kernel, heads, capacity),
        in_specs=[VMEM, SMEM],
        out_specs=VMEM,
        out_shape=jax.ShapeDtypeStruct((rows, padded), BF16),
        compiler_params=PARAMS,
        cost_estimate=cost(2 * rows * rows * 128, 2 * rows * padded),
        name="back_places",
    )(inst, owner_slot)
    effective = pl.pallas_call(
        effective_kernel,
        in_specs=[VMEM, VMEM],
        out_specs=VMEM,
        out_shape=jax.ShapeDtypeStruct((width, channels), BF16),
        compiler_params=PARAMS,
        cost_estimate=cost(width * channels, 4 * width * channels),
        name="effective",
    )(head_weights[0], mask)

    size = padded // cut
    row_grad, residual = pl.pallas_call(
        functools.partial(head_kernel, width),
        grid=(cut,),
        in_specs=[
            pl.BlockSpec((size, wide), lambda i: (i, 0)),
            whole((width, channels)),
            whole((1, channels)),
        ],
        out_specs=[
            pl.BlockSpec((size, width), lambda i: (i, 0)),
            pl.BlockSpec((size, channels), lambda i: (i, 0)),
        ],
        out_shape=[
            jax.ShapeDtypeStruct((padded, width), BF16),
            jax.ShapeDtypeStruct((padded, channels), BF16),
        ],
        compiler_params=PARAMS,
        cost_estimate=cost(4 * padded * width * channels, 2 * padded * (2 * wide + width)),
        name="heads",
    )(got, effective, error_weight)
    returned = lax.all_to_all(row_grad, "loc", split_axis=0, concat_axis=0, tiled=True)

    tall = 256
    raw_grad, squares = pl.pallas_call(
        raw_kernel,
        grid=(width // tall,),
        in_specs=[
            pl.BlockSpec((padded, tall), lambda i: (0, i)),
            whole((padded, channels)),
            whole(mask.shape),
        ],
        out_specs=[pl.BlockSpec((tall, channels), lambda i: (i, 0)), whole((8, 128))],
        out_shape=[
            jax.ShapeDtypeStruct((width, channels), F32),
            jax.ShapeDtypeStruct((8, 128), F32),
        ],
        compiler_params=PARAMS,
        cost_estimate=cost(2 * padded * width * channels, 4 * width * channels),
        name="raw_grad",
    )(got, residual, mask)
    step = members // 2
    while step:
        squares = squares + lax.ppermute(squares, "loc", [(i, i ^ step) for i in range(members)])
        step //= 2
    head_grad = pl.pallas_call(
        functools.partial(scale_kernel, math.sqrt(heads * width * channels)),
        grid=(cut,),
        in_specs=[
            pl.BlockSpec((width // cut, channels), lambda i: (i, 0)),
            whole((8, 128)),
        ],
        out_specs=pl.BlockSpec((1, width // cut, channels), lambda i: (0, i, 0)),
        out_shape=jax.ShapeDtypeStruct((1, width, channels), F32),
        compiler_params=PARAMS,
        cost_estimate=cost(width * channels, 8 * width * channels),
        name="scale",
    )(raw_grad, squares)
    latent_grad = pl.pallas_call(
        place_back_kernel,
        grid=(cut,),
        in_specs=[whole((rows, padded)), pl.BlockSpec((padded, width // cut), lambda i: (0, i))],
        out_specs=pl.BlockSpec((rows, width // cut), lambda i: (0, i)),
        out_shape=jax.ShapeDtypeStruct((rows, width), BF16),
        compiler_params=PARAMS,
        cost_estimate=cost(2 * rows * padded * width, 4 * padded * width),
        name="place_back",
    )(back, returned)
    return (latent_grad, head_grad)


def solution(mesh):
    in_specs = (
        P(("grp", "loc"), None),
        P(("grp", "loc"), None),
        P(),
        P("loc", None, None),
        P("loc", None),
        P("loc", None, None),
        P(("grp", "loc"), None),
    )
    out_specs = (P(("grp", "loc"), None), P(("grp", "loc"), None, None))
    return jax.shard_map(
        per_device, mesh=mesh, in_specs=in_specs, out_specs=out_specs, check_vma=False
    )
```

```python
import functools
import math

import jax
import jax.numpy as jnp
from jax import lax
from jax.experimental import pallas as pl
from jax.experimental.pallas import tpu as pltpu
from jax.sharding import PartitionSpec as P

BLK = 128
F32 = jnp.float32
BF16 = jnp.bfloat16
VMEM = pl.BlockSpec(memory_space=pltpu.VMEM)
SMEM = pl.BlockSpec(memory_space=pltpu.SMEM)
PARAMS = pltpu.CompilerParams(vmem_limit_bytes=60 * 1024 * 1024)


def dot(a, b, ca=1, cb=0):
    return lax.dot_general(a, b, (((ca,), (cb,)), ((), ())), preferred_element_type=F32)


def cost(flops, nbytes):
    return pl.CostEstimate(flops=int(flops), bytes_accessed=int(nbytes), transcendentals=0)


def places(inst, owner_ref, heads):
    rows = inst.shape[1]
    slot = jnp.zeros_like(inst)
    for k in range(heads):
        slot = jnp.where(inst == k, owner_ref[k], slot)
    hit = lax.broadcasted_iota(jnp.int32, (heads, rows), 0) == slot
    upto = lax.broadcasted_iota(jnp.int32, (rows, rows), 0) <= lax.broadcasted_iota(
        jnp.int32, (rows, rows), 1
    )
    count = dot(hit.astype(BF16), upto.astype(BF16))
    rank = jnp.sum(jnp.where(hit, count, 0.0), 0, keepdims=True).astype(jnp.int32) - 1
    return slot, rank


def one_hot_rows(pos, start, size):
    number = lax.broadcasted_iota(jnp.int32, (size, pos.shape[1]), 0) + start
    return (number == pos).astype(F32).astype(BF16)


def one_hot_back(pos, size):
    column = jnp.transpose(jnp.broadcast_to(pos.astype(F32), (128, pos.shape[1])))[:, :1]
    number = lax.broadcasted_iota(jnp.int32, (pos.shape[1], size), 1)
    return (number == column.astype(jnp.int32)).astype(F32).astype(BF16)


def prep_kernel(heads, capacity, inst_ref, owner_ref, x_ref, t_ref, out_ref, place_ref):
    size, width = out_ref.shape[0], x_ref.shape[1]
    step = pl.program_id(0)

    @pl.when(step == 0)
    def _():
        slot, rank = places(inst_ref[...], owner_ref, heads)
        place_ref[...] = jnp.broadcast_to(slot * capacity + rank, place_ref.shape)

    pick = one_hot_rows(place_ref[0:1, :], step * size, size)
    out_ref[:, :width] = dot(pick, x_ref[...]).astype(BF16)
    out_ref[:, width:] = dot(pick, t_ref[...]).astype(BF16)


def back_kernel(heads, capacity, inst_ref, owner_ref, back_ref):
    slot, rank = places(inst_ref[...], owner_ref, heads)
    back_ref[...] = one_hot_back(slot * capacity + rank, back_ref.shape[1])


def effective_kernel(w_ref, mask_ref, out_ref):
    for block in range(mask_ref.shape[0]):
        here = slice(block * BLK, (block + 1) * BLK)
        out_ref[here, :] = (w_ref[here, :].astype(F32) * mask_ref[block : block + 1, :]).astype(BF16)


def head_kernel(width, x_ref, eff_ref, weight_ref, grad_ref, res_ref):
    predicted = dot(x_ref[:, :width], eff_ref[...])
    residual = (weight_ref[...] * (predicted - x_ref[:, width:].astype(F32))).astype(BF16)
    res_ref[...] = residual
    grad_ref[...] = dot(residual, eff_ref[...], 1, 1).astype(BF16)


def raw_kernel(x_ref, res_ref, mask_ref, raw_ref, square_ref):
    step = pl.program_id(0)
    size, channels = raw_ref.shape
    raw = dot(x_ref[...], res_ref[...], 0, 0)

    @pl.when(step == 0)
    def _():
        square_ref[...] = jnp.zeros_like(square_ref)

    for block in range(size // BLK):
        here = slice(block * BLK, (block + 1) * BLK)
        part = raw[here, :] * mask_ref[pl.ds(step * (size // BLK) + block, 1), :]
        raw_ref[here, :] = part
        total = jnp.sum((part * part).reshape(BLK // 8, 8, channels), 0)
        for lane in range(channels // 128):
            square_ref[...] += total[:, lane * 128 : (lane + 1) * 128]


def scale_kernel(limit, raw_ref, square_ref, out_ref):
    squares = jnp.sum(square_ref[...], keepdims=True)
    factor = jnp.minimum(1.0, limit / jnp.sqrt(squares + 1e-06))
    out_ref[...] = (raw_ref[...] * factor)[None]


def place_back_kernel(back_ref, got_ref, out_ref):
    out_ref[...] = dot(back_ref[...], got_ref[...]).astype(BF16)


def per_device(latents, obs_inst, owner_slot, head_weights, error_weight, block_pattern, targets):
    members = lax.axis_size("loc")
    local_heads, width, channels = head_weights.shape
    heads = local_heads * members
    rows = latents.shape[0]
    capacity = 2 * rows // heads
    padded = heads * capacity
    wide = width + channels
    inst = obs_inst.reshape(1, rows)
    mask = jnp.repeat(block_pattern[0], BLK, 1).astype(F32)

    def whole(shape):
        return pl.BlockSpec(shape, lambda i: (0, 0))

    cut = 4
    send = pl.pallas_call(
        functools.partial(prep_kernel, heads, capacity),
        grid=(cut,),
        in_specs=[whole((1, rows)), SMEM, whole((rows, width)), whole((rows, channels))],
        out_specs=pl.BlockSpec((padded // cut, wide), lambda i: (i, 0)),
        out_shape=jax.ShapeDtypeStruct((padded, wide), BF16),
        scratch_shapes=[pltpu.VMEM((8, rows), jnp.int32)],
        compiler_params=PARAMS,
        cost_estimate=cost(2 * padded * rows * wide, 2 * (padded + rows) * wide),
        name="prep",
    )(inst, owner_slot, latents, targets)
    got = lax.all_to_all(send, "loc", split_axis=0, concat_axis=0, tiled=True)

    back = pl.pallas_call(
        functools.partial(back_kernel, heads, capacity),
        in_specs=[VMEM, SMEM],
        out_specs=VMEM,
        out_shape=jax.ShapeDtypeStruct((rows, padded), BF16),
        compiler_params=PARAMS,
        cost_estimate=cost(2 * rows * rows * 128, 2 * rows * padded),
        name="back_places",
    )(inst, owner_slot)
    effective = pl.pallas_call(
        effective_kernel,
        in_specs=[VMEM, VMEM],
        out_specs=VMEM,
        out_shape=jax.ShapeDtypeStruct((width, channels), BF16),
        compiler_params=PARAMS,
        cost_estimate=cost(width * channels, 4 * width * channels),
        name="effective",
    )(head_weights[0], mask)

    got, back, effective = lax.optimization_barrier((got, back, effective))
    size = padded // cut
    row_grad, residual = pl.pallas_call(
        functools.partial(head_kernel, width),
        grid=(cut,),
        in_specs=[
            pl.BlockSpec((size, wide), lambda i: (i, 0)),
            whole((width, channels)),
            whole((1, channels)),
        ],
        out_specs=[
            pl.BlockSpec((size, width), lambda i: (i, 0)),
            pl.BlockSpec((size, channels), lambda i: (i, 0)),
        ],
        out_shape=[
            jax.ShapeDtypeStruct((padded, width), BF16),
            jax.ShapeDtypeStruct((padded, channels), BF16),
        ],
        compiler_params=PARAMS,
        cost_estimate=cost(4 * padded * width * channels, 2 * padded * (2 * wide + width)),
        name="heads",
    )(got, effective, error_weight)
    returned = lax.all_to_all(row_grad, "loc", split_axis=0, concat_axis=0, tiled=True)

    tall = 256
    raw_grad, squares = pl.pallas_call(
        raw_kernel,
        grid=(width // tall,),
        in_specs=[
            pl.BlockSpec((padded, tall), lambda i: (0, i)),
            whole((padded, channels)),
            whole(mask.shape),
        ],
        out_specs=[pl.BlockSpec((tall, channels), lambda i: (i, 0)), whole((8, 128))],
        out_shape=[
            jax.ShapeDtypeStruct((width, channels), F32),
            jax.ShapeDtypeStruct((8, 128), F32),
        ],
        compiler_params=PARAMS,
        cost_estimate=cost(2 * padded * width * channels, 4 * width * channels),
        name="raw_grad",
    )(got, residual, mask)
    step = 1
    while step < members:
        squares = squares + lax.ppermute(squares, "loc", [(i, i ^ step) for i in range(members)])
        step *= 2
    latent_grad = pl.pallas_call(
        place_back_kernel,
        grid=(cut,),
        in_specs=[whole((rows, padded)), pl.BlockSpec((padded, width // cut), lambda i: (0, i))],
        out_specs=pl.BlockSpec((rows, width // cut), lambda i: (0, i)),
        out_shape=jax.ShapeDtypeStruct((rows, width), BF16),
        compiler_params=PARAMS,
        cost_estimate=cost(2 * rows * padded * width, 4 * padded * width),
        name="place_back",
    )(back, returned)
    latent_grad, squares = lax.optimization_barrier((latent_grad, squares))
    head_grad = pl.pallas_call(
        functools.partial(scale_kernel, math.sqrt(heads * width * channels)),
        grid=(cut,),
        in_specs=[
            pl.BlockSpec((width // cut, channels), lambda i: (i, 0)),
            whole((8, 128)),
        ],
        out_specs=pl.BlockSpec((1, width // cut, channels), lambda i: (0, i, 0)),
        out_shape=jax.ShapeDtypeStruct((1, width, channels), F32),
        compiler_params=PARAMS,
        cost_estimate=cost(width * channels, 8 * width * channels),
        name="scale",
    )(raw_grad, squares)
    return (latent_grad, head_grad)


def solution(mesh):
    in_specs = (
        P(("grp", "loc"), None),
        P(("grp", "loc"), None),
        P(),
        P("loc", None, None),
        P("loc", None),
        P("loc", None, None),
        P(("grp", "loc"), None),
    )
    out_specs = (P(("grp", "loc"), None), P(("grp", "loc"), None, None))
    return jax.shard_map(
        per_device, mesh=mesh, in_specs=in_specs, out_specs=out_specs, check_vma=False
    )
```

```python
import functools
import math

import jax
import jax.numpy as jnp
from jax import lax
from jax.experimental import pallas as pl
from jax.experimental.pallas import tpu as pltpu
from jax.sharding import PartitionSpec as P


BLK = 128
CHUNKS = 2
F32 = jnp.float32
BF16 = jnp.bfloat16
VMEM = pl.BlockSpec(memory_space=pltpu.VMEM)
SMEM = pl.BlockSpec(memory_space=pltpu.SMEM)
STREAM = pltpu.CompilerParams(vmem_limit_bytes=60 * 1024 * 1024)
SMALL = pltpu.CompilerParams(vmem_limit_bytes=32 * 1024 * 1024)


def dot(a, b, ca=1, cb=0):
    return lax.dot_general(a, b, (((ca,), (cb,)), ((), ())), preferred_element_type=F32)


def cost(flops, nbytes):
    return pl.CostEstimate(flops=int(flops), bytes_accessed=int(nbytes), transcendentals=0)


def whole(shape):
    return pl.BlockSpec(shape, lambda i: (0,) * len(shape))


def places(inst, owner_ref, heads):
    rows = inst.shape[1]
    slot = jnp.zeros_like(inst)
    for k in range(heads):
        slot = jnp.where(inst == k, owner_ref[k], slot)
    hit = lax.broadcasted_iota(jnp.int32, (heads, rows), 0) == slot
    upto = lax.broadcasted_iota(jnp.int32, (rows, rows), 0) <= lax.broadcasted_iota(
        jnp.int32, (rows, rows), 1
    )
    count = dot(hit.astype(BF16), upto.astype(BF16))
    rank = jnp.sum(jnp.where(hit, count, 0.0), 0, keepdims=True).astype(jnp.int32) - 1
    return slot, rank


def half_places(inst, owner_ref, heads, capacity):
    slot, rank = places(inst, owner_ref, heads)
    half = heads // 2
    mine = (slot >= half) == (lax.axis_index("loc") >= half)
    place = jnp.where(slot >= half, slot - half, slot) * capacity + rank
    return jnp.where(mine, place, -1), jnp.where(mine, -1, place)


def one_hot_back(pos, size):
    column = jnp.transpose(jnp.broadcast_to(pos.astype(F32), (128, pos.shape[1])))[:, :1]
    number = lax.broadcasted_iota(jnp.int32, (pos.shape[1], size), 1)
    return (number == column.astype(jnp.int32)).astype(F32).astype(BF16)


def prep_kernel(heads, capacity, which, inst_ref, owner_ref, x_ref, t_ref, out_ref, place_ref):
    size, width = out_ref.shape[0], x_ref.shape[1]
    step = pl.program_id(0)

    @pl.when(step == 0)
    def _():
        place = half_places(inst_ref[...], owner_ref, heads, capacity)[which]
        place_ref[...] = jnp.broadcast_to(place, place_ref.shape)

    number = lax.broadcasted_iota(jnp.int32, (size, inst_ref.shape[1]), 0) + step * size
    pick = (number == place_ref[0:1, :]).astype(F32).astype(BF16)
    out_ref[:, :width] = dot(pick, x_ref[...]).astype(BF16)
    out_ref[:, width:] = dot(pick, t_ref[...]).astype(BF16)


def back_kernel(heads, capacity, inst_ref, owner_ref, near_ref, far_ref):
    near, far = half_places(inst_ref[...], owner_ref, heads, capacity)
    near_ref[...] = one_hot_back(near, near_ref.shape[1])
    far_ref[...] = one_hot_back(far, far_ref.shape[1])


def masked(block, pattern_ref, row, column):
    return (block.astype(F32) * pattern_ref[0, row, column].astype(F32)).astype(BF16)


def piece_kernel(w_ref, pattern_ref, *out_refs):
    rows, channels = out_refs[0].shape
    for chunk, out_ref in enumerate(out_refs):
        first = (lax.axis_index("grp") * len(out_refs) + chunk) * (rows // BLK)
        for i in range(rows // BLK):
            here = pl.ds(pl.multiple_of((first + i) * BLK, BLK), BLK)
            for j in range(channels // BLK):
                cols = slice(j * BLK, (j + 1) * BLK)
                out_ref[i * BLK : (i + 1) * BLK, cols] = masked(
                    w_ref[0, here, cols], pattern_ref, first + i, j
                )


def effective_kernel(w_ref, pattern_ref, out_ref):
    width, channels = out_ref.shape
    for i in range(width // BLK):
        for j in range(channels // BLK):
            rows, cols = slice(i * BLK, (i + 1) * BLK), slice(j * BLK, (j + 1) * BLK)
            out_ref[rows, cols] = masked(w_ref[0, rows, cols], pattern_ref, i, j)


def head_kernel(width, x_ref, eff_ref, weight_ref, grad_ref, res_ref):
    predicted = dot(x_ref[:, :width], eff_ref[...])
    residual = (weight_ref[...] * (predicted - x_ref[:, width:].astype(F32))).astype(BF16)
    res_ref[...] = residual
    grad_ref[...] = dot(residual, eff_ref[...], 1, 1).astype(BF16)


def far_head_kernel(width, count, x_ref, weight_ref, *refs):
    eff_refs, (grad_ref, res_ref) = refs[:count], refs[count:]
    deep = eff_refs[0].shape[0]
    group = lax.axis_index("grp")

    def columns(number):
        first = (group ^ (number // CHUNKS)) * CHUNKS + number % CHUNKS
        return pl.ds(pl.multiple_of(first * deep, deep), deep)

    predicted = dot(x_ref[:, columns(0)], eff_refs[0][...])
    for number in range(1, count):
        predicted += dot(x_ref[:, columns(number)], eff_refs[number][...])
    residual = (weight_ref[...] * (predicted - x_ref[:, width:].astype(F32))).astype(BF16)
    res_ref[...] = residual
    for number in range(count):
        grad_ref[:, columns(number)] = dot(residual, eff_refs[number][...], 1, 1).astype(BF16)


def far_raw_kernel(x_ref, res_ref, out_ref):
    out_ref[...] = dot(x_ref[...], res_ref[...], 0, 0).astype(BF16)


def raw_kernel(first, x_ref, res_ref, far_ref, pattern_ref, raw_ref, square_ref):
    step = pl.program_id(0)
    size, channels = raw_ref.shape
    raw = dot(x_ref[...], res_ref[...], 0, 0) + far_ref[...].astype(F32)

    @pl.when(step == 0)
    def _():
        square_ref[...] = jnp.zeros_like(square_ref)

    for i in range(size // BLK):
        for j in range(channels // BLK):
            rows, cols = slice(i * BLK, (i + 1) * BLK), slice(j * BLK, (j + 1) * BLK)
            used = pattern_ref[0, first + step * (size // BLK) + i, j].astype(F32)
            part = raw[rows, cols] * used
            raw_ref[rows, cols] = part
            square_ref[...] += jnp.sum((part * part).reshape(BLK // 8, 8, BLK), 0)


def scale_kernel(limit, parts, *refs):
    raw_refs, square_ref, out_ref = refs[:parts], refs[parts], refs[parts + 1]
    squares = jnp.sum(square_ref[...], keepdims=True)
    factor = jnp.minimum(1.0, limit / jnp.sqrt(squares + 1e-06))
    step = pl.program_id(0)
    per = pl.num_programs(0) // parts
    for part in range(parts):

        @pl.when(step // per == part)
        def _():
            out_ref[...] = (raw_refs[part][...] * factor)[None]


def place_back_kernel(near_ref, far_ref, near_got_ref, far_got_ref, out_ref):
    out = dot(near_ref[...], near_got_ref[...]) + dot(far_ref[...], far_got_ref[...])
    out_ref[...] = out.astype(BF16)


def per_device(latents, obs_inst, owner_slot, head_weights, error_weight, block_pattern, targets):
    members, groups = lax.axis_size("loc"), lax.axis_size("grp")
    local_heads, width, channels = head_weights.shape
    heads = local_heads * members
    rows = latents.shape[0]
    capacity = 2 * rows // heads
    half = members // 2
    placed = half * capacity
    wide = width + channels
    inst = obs_inst.reshape(1, rows)
    halves = [list(range(half)), list(range(half, members))]

    def partner(x):
        return lax.ppermute(x, "loc", [(i, i ^ half) for i in range(members)])

    def in_half(x):
        return lax.all_to_all(
            x, "loc", split_axis=0, concat_axis=0, tiled=True, axis_index_groups=halves
        )

    deep = width // (groups * CHUNKS)
    pieces = pl.pallas_call(
        piece_kernel,
        in_specs=[VMEM, SMEM],
        out_specs=[VMEM] * CHUNKS,
        out_shape=[jax.ShapeDtypeStruct((deep, channels), BF16)] * CHUNKS,
        compiler_params=STREAM,
        cost_estimate=cost(CHUNKS * deep * channels, 4 * CHUNKS * deep * channels),
        name="piece",
    )(head_weights, block_pattern)
    inst, pieces = lax.optimization_barrier((inst, pieces))
    far_weight = partner(error_weight)
    swapped = [[partner(piece)] for piece in pieces]
    step = 1
    while step < groups:
        swap = [(i, i ^ step) for i in range(groups)]
        swapped = [held + [lax.ppermute(x, "grp", swap) for x in held] for held in swapped]
        step *= 2
    far_eff = [swapped[chunk][number] for number in range(groups) for chunk in range(CHUNKS)]

    cut = 4

    def prep(which, name):
        return pl.pallas_call(
            functools.partial(prep_kernel, heads, capacity, which),
            grid=(cut,),
            in_specs=[whole((1, rows)), SMEM, whole((rows, width)), whole((rows, channels))],
            out_specs=pl.BlockSpec((placed // cut, wide), lambda i: (i, 0)),
            out_shape=jax.ShapeDtypeStruct((placed, wide), BF16),
            scratch_shapes=[pltpu.VMEM((8, rows), jnp.int32)],
            compiler_params=STREAM,
            cost_estimate=cost(2 * placed * rows * wide, 2 * (placed + rows) * wide),
            name=name,
        )(inst, owner_slot, latents, targets)

    far_x = in_half(prep(1, "prep_far"))
    near_send = prep(0, "prep_near")
    near_send, far_x = lax.optimization_barrier((near_send, far_x))
    near_x = in_half(near_send)

    near_back, far_back = pl.pallas_call(
        functools.partial(back_kernel, heads, capacity),
        in_specs=[VMEM, SMEM],
        out_specs=[VMEM, VMEM],
        out_shape=[jax.ShapeDtypeStruct((rows, placed), BF16)] * 2,
        compiler_params=STREAM,
        cost_estimate=cost(2 * rows * rows * 128, 4 * rows * placed),
        name="back_places",
    )(inst, owner_slot)
    effective = pl.pallas_call(
        effective_kernel,
        in_specs=[VMEM, SMEM],
        out_specs=VMEM,
        out_shape=jax.ShapeDtypeStruct((width, channels), BF16),
        compiler_params=STREAM,
        cost_estimate=cost(width * channels, 4 * width * channels),
        name="effective",
    )(head_weights, block_pattern)

    size = placed // cut
    head_out = [
        pl.BlockSpec((size, width), lambda i: (i, 0)),
        pl.BlockSpec((size, channels), lambda i: (i, 0)),
    ]
    head_shape = [
        jax.ShapeDtypeStruct((placed, width), BF16),
        jax.ShapeDtypeStruct((placed, channels), BF16),
    ]
    head_cost = cost(4 * placed * width * channels, 2 * placed * (2 * wide + width))
    row_spec = pl.BlockSpec((size, wide), lambda i: (i, 0))
    far_grad, far_res = pl.pallas_call(
        functools.partial(far_head_kernel, width, len(far_eff)),
        grid=(cut,),
        in_specs=[row_spec, whole((1, channels))] + [whole((deep, channels))] * len(far_eff),
        out_specs=head_out,
        out_shape=head_shape,
        compiler_params=STREAM,
        cost_estimate=head_cost,
        name="far_head",
    )(far_x, far_weight, *far_eff)

    tall = 256
    steps = width // (CHUNKS * tall)
    far_raw = []
    for chunk in range(CHUNKS):
        part = pl.pallas_call(
            far_raw_kernel,
            grid=(steps,),
            in_specs=[
                pl.BlockSpec((placed, tall), lambda i, chunk=chunk: (0, chunk * steps + i)),
                whole((placed, channels)),
            ],
            out_specs=pl.BlockSpec((tall, channels), lambda i: (i, 0)),
            out_shape=jax.ShapeDtypeStruct((width // CHUNKS, channels), BF16),
            compiler_params=STREAM,
            cost_estimate=cost(2 * placed * width * channels // CHUNKS, 2 * width * channels),
            name="far_raw",
        )(far_x, far_res)
        far_raw.append(partner(part))

    near_x, effective, near_back, far_back = lax.optimization_barrier(
        (near_x, effective, near_back, far_back)
    )
    near_grad, near_res = pl.pallas_call(
        functools.partial(head_kernel, width),
        grid=(cut,),
        in_specs=[row_spec, whole((width, channels)), whole((1, channels))],
        out_specs=head_out,
        out_shape=head_shape,
        compiler_params=STREAM,
        cost_estimate=head_cost,
        name="near_head",
    )(near_x, effective, error_weight)

    far_got = in_half(far_grad)
    near_grad, far_got = lax.optimization_barrier((near_grad, far_got))
    near_got = in_half(near_grad)
    latent_grad = pl.pallas_call(
        place_back_kernel,
        grid=(cut,),
        in_specs=[whole((rows, placed))] * 2
        + [pl.BlockSpec((placed, width // cut), lambda i: (0, i))] * 2,
        out_specs=pl.BlockSpec((rows, width // cut), lambda i: (0, i)),
        out_shape=jax.ShapeDtypeStruct((rows, width), BF16),
        compiler_params=STREAM,
        cost_estimate=cost(4 * rows * placed * width, 8 * placed * width),
        name="place_back",
    )(near_back, far_back, near_got, far_got)

    raw_grad, squares = [], 0.0
    for chunk in range(CHUNKS):
        part, square = pl.pallas_call(
            functools.partial(raw_kernel, chunk * steps * (tall // BLK)),
            grid=(steps,),
            in_specs=[
                pl.BlockSpec((placed, tall), lambda i, chunk=chunk: (0, chunk * steps + i)),
                whole((placed, channels)),
                pl.BlockSpec((tall, channels), lambda i: (i, 0)),
                SMEM,
            ],
            out_specs=[pl.BlockSpec((tall, channels), lambda i: (i, 0)), whole((8, 128))],
            out_shape=[
                jax.ShapeDtypeStruct((width // CHUNKS, channels), F32),
                jax.ShapeDtypeStruct((8, 128), F32),
            ],
            compiler_params=SMALL,
            cost_estimate=cost(2 * placed * width * channels // CHUNKS, 4 * width * channels),
            name="raw",
        )(near_x, near_res, far_raw[chunk], block_pattern)
        raw_grad.append(part)
        squares = squares + square
    step = 1
    while step < members:
        squares = squares + lax.ppermute(squares, "loc", [(i, i ^ step) for i in range(members)])
        step *= 2

    def raw_spec(part):
        low = part * (cut // CHUNKS)
        return pl.BlockSpec(
            (width // cut, channels), lambda i: (jnp.clip(i - low, 0, cut // CHUNKS - 1), 0)
        )

    head_grad = pl.pallas_call(
        functools.partial(scale_kernel, math.sqrt(heads * width * channels), CHUNKS),
        grid=(cut,),
        in_specs=[raw_spec(part) for part in range(CHUNKS)] + [whole((8, 128))],
        out_specs=pl.BlockSpec((1, width // cut, channels), lambda i: (0, i, 0)),
        out_shape=jax.ShapeDtypeStruct((1, width, channels), F32),
        compiler_params=SMALL,
        cost_estimate=cost(width * channels, 8 * width * channels),
        name="scale",
    )(*raw_grad, squares)
    return (latent_grad, head_grad)


def solution(mesh):
    in_specs = (
        P(("grp", "loc"), None),
        P(("grp", "loc"), None),
        P(),
        P("loc", None, None),
        P("loc", None),
        P("loc", None, None),
        P(("grp", "loc"), None),
    )
    out_specs = (P(("grp", "loc"), None), P(("grp", "loc"), None, None))
    return jax.shard_map(
        per_device, mesh=mesh, in_specs=in_specs, out_specs=out_specs, check_vma=False
    )
```

```python
import functools
import math

import jax
import jax.numpy as jnp
from jax import lax
from jax.experimental import pallas as pl
from jax.experimental.pallas import tpu as pltpu
from jax.sharding import PartitionSpec as P


BLK = 128
CHUNKS = 2
F32 = jnp.float32
BF16 = jnp.bfloat16
VMEM = pl.BlockSpec(memory_space=pltpu.VMEM)
SMEM = pl.BlockSpec(memory_space=pltpu.SMEM)
STREAM = pltpu.CompilerParams(vmem_limit_bytes=60 * 1024 * 1024)
SMALL = pltpu.CompilerParams(vmem_limit_bytes=32 * 1024 * 1024)


def dot(a, b, ca=1, cb=0):
    return lax.dot_general(a, b, (((ca,), (cb,)), ((), ())), preferred_element_type=F32)


def cost(flops, nbytes):
    return pl.CostEstimate(flops=int(flops), bytes_accessed=int(nbytes), transcendentals=0)


def whole(shape):
    return pl.BlockSpec(shape, lambda i: (0,) * len(shape))


def places(inst, owner_ref, heads):
    rows = inst.shape[1]
    slot = jnp.zeros_like(inst)
    for k in range(heads):
        slot = jnp.where(inst == k, owner_ref[k], slot)
    hit = lax.broadcasted_iota(jnp.int32, (heads, rows), 0) == slot
    upto = lax.broadcasted_iota(jnp.int32, (rows, rows), 0) <= lax.broadcasted_iota(
        jnp.int32, (rows, rows), 1
    )
    count = dot(hit.astype(BF16), upto.astype(BF16))
    rank = jnp.sum(jnp.where(hit, count, 0.0), 0, keepdims=True).astype(jnp.int32) - 1
    return slot, rank


def half_places(inst, owner_ref, heads, capacity):
    slot, rank = places(inst, owner_ref, heads)
    half = heads // 2
    mine = (slot >= half) == (lax.axis_index("loc") >= half)
    place = jnp.where(slot >= half, slot - half, slot) * capacity + rank
    return jnp.where(mine, place, -1), jnp.where(mine, -1, place)


def one_hot_back(pos, size):
    column = jnp.transpose(jnp.broadcast_to(pos.astype(F32), (128, pos.shape[1])))[:, :1]
    number = lax.broadcasted_iota(jnp.int32, (pos.shape[1], size), 1)
    return (number == column.astype(jnp.int32)).astype(F32).astype(BF16)


def prep_kernel(heads, capacity, which, inst_ref, owner_ref, x_ref, t_ref, out_ref, place_ref):
    size, width = out_ref.shape[0], x_ref.shape[1]
    step = pl.program_id(0)

    @pl.when(step == 0)
    def _():
        place = half_places(inst_ref[...], owner_ref, heads, capacity)[which]
        place_ref[...] = jnp.broadcast_to(place, place_ref.shape)

    number = lax.broadcasted_iota(jnp.int32, (size, inst_ref.shape[1]), 0) + step * size
    pick = (number == place_ref[0:1, :]).astype(F32).astype(BF16)
    out_ref[:, :width] = dot(pick, x_ref[...]).astype(BF16)
    out_ref[:, width:] = dot(pick, t_ref[...]).astype(BF16)


def back_kernel(heads, capacity, inst_ref, owner_ref, near_ref, far_ref):
    near, far = half_places(inst_ref[...], owner_ref, heads, capacity)
    near_ref[...] = one_hot_back(near, near_ref.shape[1])
    far_ref[...] = one_hot_back(far, far_ref.shape[1])


def masked(block, pattern_ref, row, column):
    return (block.astype(F32) * pattern_ref[0, row, column].astype(F32)).astype(BF16)


def piece_kernel(w_ref, pattern_ref, *out_refs):
    rows, channels = out_refs[0].shape
    for chunk, out_ref in enumerate(out_refs):
        first = (lax.axis_index("grp") * len(out_refs) + chunk) * (rows // BLK)
        for i in range(rows // BLK):
            here = pl.ds(pl.multiple_of((first + i) * BLK, BLK), BLK)
            for j in range(channels // BLK):
                cols = slice(j * BLK, (j + 1) * BLK)
                out_ref[i * BLK : (i + 1) * BLK, cols] = masked(
                    w_ref[0, here, cols], pattern_ref, first + i, j
                )


def effective_kernel(w_ref, pattern_ref, out_ref):
    width, channels = out_ref.shape
    for i in range(width // BLK):
        for j in range(channels // BLK):
            rows, cols = slice(i * BLK, (i + 1) * BLK), slice(j * BLK, (j + 1) * BLK)
            out_ref[rows, cols] = masked(w_ref[0, rows, cols], pattern_ref, i, j)


def head_kernel(width, x_ref, eff_ref, weight_ref, grad_ref, res_ref):
    predicted = dot(x_ref[:, :width], eff_ref[...])
    residual = (weight_ref[...] * (predicted - x_ref[:, width:].astype(F32))).astype(BF16)
    res_ref[...] = residual
    grad_ref[...] = dot(residual, eff_ref[...], 1, 1).astype(BF16)


def far_head_kernel(width, count, x_ref, weight_ref, *refs):
    eff_refs, (grad_ref, res_ref) = refs[:count], refs[count:]
    deep = eff_refs[0].shape[0]
    group = lax.axis_index("grp")

    def columns(number):
        first = (group ^ (number // CHUNKS)) * CHUNKS + number % CHUNKS
        return pl.ds(pl.multiple_of(first * deep, deep), deep)

    predicted = dot(x_ref[:, columns(0)], eff_refs[0][...])
    for number in range(1, count):
        predicted += dot(x_ref[:, columns(number)], eff_refs[number][...])
    residual = (weight_ref[...] * (predicted - x_ref[:, width:].astype(F32))).astype(BF16)
    res_ref[...] = residual
    for number in range(count):
        grad_ref[:, columns(number)] = dot(residual, eff_refs[number][...], 1, 1).astype(BF16)


def far_raw_kernel(x_ref, res_ref, out_ref):
    out_ref[...] = dot(x_ref[...], res_ref[...], 0, 0).astype(BF16)


def raw_kernel(first, x_ref, res_ref, far_ref, pattern_ref, raw_ref, square_ref):
    step = pl.program_id(0)
    size, channels = raw_ref.shape
    raw = dot(x_ref[...], res_ref[...], 0, 0) + far_ref[...].astype(F32)

    @pl.when(step == 0)
    def _():
        square_ref[...] = jnp.zeros_like(square_ref)

    for i in range(size // BLK):
        for j in range(channels // BLK):
            rows, cols = slice(i * BLK, (i + 1) * BLK), slice(j * BLK, (j + 1) * BLK)
            used = pattern_ref[0, first + step * (size // BLK) + i, j].astype(F32)
            part = raw[rows, cols] * used
            raw_ref[rows, cols] = part
            square_ref[...] += jnp.sum((part * part).reshape(BLK // 8, 8, BLK), 0)


def scale_kernel(limit, parts, *refs):
    raw_refs, square_ref, out_ref = refs[:parts], refs[parts], refs[parts + 1]
    squares = jnp.sum(square_ref[...], keepdims=True)
    factor = jnp.minimum(1.0, limit / jnp.sqrt(squares + 1e-06))
    step = pl.program_id(0)
    per = pl.num_programs(0) // parts
    for part in range(parts):

        @pl.when(step // per == part)
        def _():
            out_ref[...] = (raw_refs[part][...] * factor)[None]


def place_back_kernel(near_ref, far_ref, near_got_ref, far_got_ref, out_ref):
    out = dot(near_ref[...], near_got_ref[...]) + dot(far_ref[...], far_got_ref[...])
    out_ref[...] = out.astype(BF16)


def per_device(latents, obs_inst, owner_slot, head_weights, error_weight, block_pattern, targets):
    members, groups = lax.axis_size("loc"), lax.axis_size("grp")
    local_heads, width, channels = head_weights.shape
    heads = local_heads * members
    rows = latents.shape[0]
    capacity = 2 * rows // heads
    half = members // 2
    placed = half * capacity
    wide = width + channels
    inst = obs_inst.reshape(1, rows)
    halves = [list(range(half)), list(range(half, members))]

    def partner(x):
        return lax.ppermute(x, "loc", [(i, i ^ half) for i in range(members)])

    def in_half(x):
        return lax.all_to_all(
            x, "loc", split_axis=0, concat_axis=0, tiled=True, axis_index_groups=halves
        )

    deep = width // (groups * CHUNKS)
    pieces = pl.pallas_call(
        piece_kernel,
        in_specs=[VMEM, SMEM],
        out_specs=[VMEM] * CHUNKS,
        out_shape=[jax.ShapeDtypeStruct((deep, channels), BF16)] * CHUNKS,
        compiler_params=STREAM,
        cost_estimate=cost(CHUNKS * deep * channels, 4 * CHUNKS * deep * channels),
        name="piece",
    )(head_weights, block_pattern)
    inst, pieces = lax.optimization_barrier((inst, pieces))
    far_weight = partner(error_weight)
    swapped = [[partner(piece)] for piece in pieces]
    step = 1
    while step < groups:
        swap = [(i, i ^ step) for i in range(groups)]
        swapped = [held + [lax.ppermute(x, "grp", swap) for x in held] for held in swapped]
        step *= 2
    far_eff = [swapped[chunk][number] for number in range(groups) for chunk in range(CHUNKS)]

    cut = 4

    def prep(which, name):
        return pl.pallas_call(
            functools.partial(prep_kernel, heads, capacity, which),
            grid=(cut,),
            in_specs=[whole((1, rows)), SMEM, whole((rows, width)), whole((rows, channels))],
            out_specs=pl.BlockSpec((placed // cut, wide), lambda i: (i, 0)),
            out_shape=jax.ShapeDtypeStruct((placed, wide), BF16),
            scratch_shapes=[pltpu.VMEM((8, rows), jnp.int32)],
            compiler_params=STREAM,
            cost_estimate=cost(2 * placed * rows * wide, 2 * (placed + rows) * wide),
            name=name,
        )(inst, owner_slot, latents, targets)

    far_x = in_half(prep(1, "prep_far"))
    near_send = prep(0, "prep_near")
    crossed = [held[0] for held in swapped]
    near_send, far_x, crossed = lax.optimization_barrier((near_send, far_x, crossed))
    near_x = in_half(near_send)

    near_back, far_back = pl.pallas_call(
        functools.partial(back_kernel, heads, capacity),
        in_specs=[VMEM, SMEM],
        out_specs=[VMEM, VMEM],
        out_shape=[jax.ShapeDtypeStruct((rows, placed), BF16)] * 2,
        compiler_params=STREAM,
        cost_estimate=cost(2 * rows * rows * 128, 4 * rows * placed),
        name="back_places",
    )(inst, owner_slot)
    effective = pl.pallas_call(
        effective_kernel,
        in_specs=[VMEM, SMEM],
        out_specs=VMEM,
        out_shape=jax.ShapeDtypeStruct((width, channels), BF16),
        compiler_params=STREAM,
        cost_estimate=cost(width * channels, 4 * width * channels),
        name="effective",
    )(head_weights, block_pattern)

    size = placed // cut
    head_out = [
        pl.BlockSpec((size, width), lambda i: (i, 0)),
        pl.BlockSpec((size, channels), lambda i: (i, 0)),
    ]
    head_shape = [
        jax.ShapeDtypeStruct((placed, width), BF16),
        jax.ShapeDtypeStruct((placed, channels), BF16),
    ]
    head_cost = cost(4 * placed * width * channels, 2 * placed * (2 * wide + width))
    row_spec = pl.BlockSpec((size, wide), lambda i: (i, 0))
    far_grad, far_res = pl.pallas_call(
        functools.partial(far_head_kernel, width, len(far_eff)),
        grid=(cut,),
        in_specs=[row_spec, whole((1, channels))] + [whole((deep, channels))] * len(far_eff),
        out_specs=head_out,
        out_shape=head_shape,
        compiler_params=STREAM,
        cost_estimate=head_cost,
        name="far_head",
    )(far_x, far_weight, *far_eff)

    tall = 256
    steps = width // (CHUNKS * tall)
    far_raw = []
    for chunk in range(CHUNKS):
        part = pl.pallas_call(
            far_raw_kernel,
            grid=(steps,),
            in_specs=[
                pl.BlockSpec((placed, tall), lambda i, chunk=chunk: (0, chunk * steps + i)),
                whole((placed, channels)),
            ],
            out_specs=pl.BlockSpec((tall, channels), lambda i: (i, 0)),
            out_shape=jax.ShapeDtypeStruct((width // CHUNKS, channels), BF16),
            compiler_params=STREAM,
            cost_estimate=cost(2 * placed * width * channels // CHUNKS, 2 * width * channels),
            name="far_raw",
        )(far_x, far_res)
        far_raw.append(part)
    sent = far_raw
    far_raw = [partner(part) for part in sent]
    far_grad, sent = lax.optimization_barrier((far_grad, sent))

    near_x, effective, near_back, far_back = lax.optimization_barrier(
        (near_x, effective, near_back, far_back)
    )
    near_grad, near_res = pl.pallas_call(
        functools.partial(head_kernel, width),
        grid=(cut,),
        in_specs=[row_spec, whole((width, channels)), whole((1, channels))],
        out_specs=head_out,
        out_shape=head_shape,
        compiler_params=STREAM,
        cost_estimate=head_cost,
        name="near_head",
    )(near_x, effective, error_weight)

    far_got = in_half(far_grad)
    near_grad, far_got = lax.optimization_barrier((near_grad, far_got))
    near_got = in_half(near_grad)
    latent_grad = pl.pallas_call(
        place_back_kernel,
        grid=(cut,),
        in_specs=[whole((rows, placed))] * 2
        + [pl.BlockSpec((placed, width // cut), lambda i: (0, i))] * 2,
        out_specs=pl.BlockSpec((rows, width // cut), lambda i: (0, i)),
        out_shape=jax.ShapeDtypeStruct((rows, width), BF16),
        compiler_params=STREAM,
        cost_estimate=cost(4 * rows * placed * width, 8 * placed * width),
        name="place_back",
    )(near_back, far_back, near_got, far_got)

    raw_grad, squares = [], 0.0
    for chunk in range(CHUNKS):
        part, square = pl.pallas_call(
            functools.partial(raw_kernel, chunk * steps * (tall // BLK)),
            grid=(steps,),
            in_specs=[
                pl.BlockSpec((placed, tall), lambda i, chunk=chunk: (0, chunk * steps + i)),
                whole((placed, channels)),
                pl.BlockSpec((tall, channels), lambda i: (i, 0)),
                SMEM,
            ],
            out_specs=[pl.BlockSpec((tall, channels), lambda i: (i, 0)), whole((8, 128))],
            out_shape=[
                jax.ShapeDtypeStruct((width // CHUNKS, channels), F32),
                jax.ShapeDtypeStruct((8, 128), F32),
            ],
            compiler_params=SMALL,
            cost_estimate=cost(2 * placed * width * channels // CHUNKS, 4 * width * channels),
            name="raw",
        )(near_x, near_res, far_raw[chunk], block_pattern)
        raw_grad.append(part)
        squares = squares + square
    latent_grad, squares = lax.optimization_barrier((latent_grad, squares))
    step = 1
    while step < members:
        squares = squares + lax.ppermute(squares, "loc", [(i, i ^ step) for i in range(members)])
        step *= 2

    def raw_spec(part):
        low = part * (cut // CHUNKS)
        return pl.BlockSpec(
            (width // cut, channels), lambda i: (jnp.clip(i - low, 0, cut // CHUNKS - 1), 0)
        )

    head_grad = pl.pallas_call(
        functools.partial(scale_kernel, math.sqrt(heads * width * channels), CHUNKS),
        grid=(cut,),
        in_specs=[raw_spec(part) for part in range(CHUNKS)] + [whole((8, 128))],
        out_specs=pl.BlockSpec((1, width // cut, channels), lambda i: (0, i, 0)),
        out_shape=jax.ShapeDtypeStruct((1, width, channels), F32),
        compiler_params=SMALL,
        cost_estimate=cost(width * channels, 8 * width * channels),
        name="scale",
    )(*raw_grad, squares)
    return (latent_grad, head_grad)


def solution(mesh):
    in_specs = (
        P(("grp", "loc"), None),
        P(("grp", "loc"), None),
        P(),
        P("loc", None, None),
        P("loc", None),
        P("loc", None, None),
        P(("grp", "loc"), None),
    )
    out_specs = (P(("grp", "loc"), None), P(("grp", "loc"), None, None))
    return jax.shard_map(
        per_device, mesh=mesh, in_specs=in_specs, out_specs=out_specs, check_vma=False
    )
```

```python
import functools
import math

import jax
import jax.numpy as jnp
from jax import lax
from jax.experimental import pallas as pl
from jax.experimental.pallas import tpu as pltpu
from jax.sharding import PartitionSpec as P


BLK = 128
CHUNKS = 4
F32 = jnp.float32
BF16 = jnp.bfloat16
VMEM = pl.BlockSpec(memory_space=pltpu.VMEM)
SMEM = pl.BlockSpec(memory_space=pltpu.SMEM)
STREAM = pltpu.CompilerParams(vmem_limit_bytes=60 * 1024 * 1024)
SMALL = pltpu.CompilerParams(vmem_limit_bytes=24 * 1024 * 1024)


def dot(a, b, ca=1, cb=0):
    return lax.dot_general(a, b, (((ca,), (cb,)), ((), ())), preferred_element_type=F32)


def cost(flops, nbytes):
    return pl.CostEstimate(flops=int(flops), bytes_accessed=int(nbytes), transcendentals=0)


def whole(shape):
    return pl.BlockSpec(shape, lambda i: (0,) * len(shape))


def places(inst, owner_ref, heads):
    rows = inst.shape[1]
    slot = jnp.zeros_like(inst)
    for k in range(heads):
        slot = jnp.where(inst == k, owner_ref[k], slot)
    hit = lax.broadcasted_iota(jnp.int32, (heads, rows), 0) == slot
    upto = lax.broadcasted_iota(jnp.int32, (rows, rows), 0) <= lax.broadcasted_iota(
        jnp.int32, (rows, rows), 1
    )
    count = dot(hit.astype(BF16), upto.astype(BF16))
    rank = jnp.sum(jnp.where(hit, count, 0.0), 0, keepdims=True).astype(jnp.int32) - 1
    return slot, rank


def half_places(inst, owner_ref, heads, capacity):
    slot, rank = places(inst, owner_ref, heads)
    half = heads // 2
    mine = (slot >= half) == (lax.axis_index("loc") >= half)
    return mine, jnp.where(slot >= half, slot - half, slot), rank


def one_hot_back(pos, size):
    column = jnp.transpose(jnp.broadcast_to(pos.astype(F32), (128, pos.shape[1])))[:, :1]
    number = lax.broadcasted_iota(jnp.int32, (pos.shape[1], size), 1)
    return (number == column.astype(jnp.int32)).astype(F32).astype(BF16)


def prep_kernel(heads, capacity, near, inst_ref, owner_ref, x_ref, t_ref, out_ref, place_ref):
    size, width = out_ref.shape[0], x_ref.shape[1]
    step = pl.program_id(0)

    @pl.when(step == 0)
    def _():
        mine, head, rank = half_places(inst_ref[...], owner_ref, heads, capacity)
        place = jnp.where(mine == near, head * capacity + rank, -1)
        place_ref[...] = jnp.broadcast_to(place, place_ref.shape)

    number = lax.broadcasted_iota(jnp.int32, (size, inst_ref.shape[1]), 0) + step * size
    pick = (number == place_ref[0:1, :]).astype(F32).astype(BF16)
    out_ref[:, :width] = dot(pick, x_ref[...]).astype(BF16)
    out_ref[:, width:] = dot(pick, t_ref[...]).astype(BF16)


def back_kernel(heads, capacity, inst_ref, owner_ref, near_ref, far_ref):
    mine, head, rank = half_places(inst_ref[...], owner_ref, heads, capacity)
    place = head * capacity + rank
    near_ref[...] = one_hot_back(jnp.where(mine, place, -1), near_ref.shape[1])
    far_ref[...] = one_hot_back(jnp.where(mine, -1, place), far_ref.shape[1])


def masked(block, pattern_ref, row, column):
    return (block.astype(F32) * pattern_ref[0, row, column].astype(F32)).astype(BF16)


def piece_kernel(w_ref, pattern_ref, *out_refs):
    rows, channels = out_refs[0].shape
    for chunk, out_ref in enumerate(out_refs):
        first = (lax.axis_index("grp") * len(out_refs) + chunk) * (rows // BLK)
        for i in range(rows // BLK):
            here = pl.ds(pl.multiple_of((first + i) * BLK, BLK), BLK)
            for j in range(channels // BLK):
                cols = slice(j * BLK, (j + 1) * BLK)
                out_ref[i * BLK : (i + 1) * BLK, cols] = masked(
                    w_ref[0, here, cols], pattern_ref, first + i, j
                )


def effective_kernel(w_ref, pattern_ref, out_ref):
    width, channels = out_ref.shape
    for i in range(width // BLK):
        for j in range(channels // BLK):
            rows, cols = slice(i * BLK, (i + 1) * BLK), slice(j * BLK, (j + 1) * BLK)
            out_ref[rows, cols] = masked(w_ref[0, rows, cols], pattern_ref, i, j)


def piece_columns(number, deep):
    first = (lax.axis_index("grp") ^ (number // CHUNKS)) * CHUNKS + number % CHUNKS
    return pl.ds(pl.multiple_of(first * deep, deep), deep)


def far_res_kernel(width, x_ref, weight_ref, *refs):
    eff_refs, res_ref = refs[:-1], refs[-1]
    deep = eff_refs[0].shape[0]
    predicted = dot(x_ref[:, piece_columns(0, deep)], eff_refs[0][...])
    for number in range(1, len(eff_refs)):
        predicted += dot(x_ref[:, piece_columns(number, deep)], eff_refs[number][...])
    misfit = predicted - x_ref[:, width:].astype(F32)
    res_ref[...] = (weight_ref[...] * misfit).astype(BF16)


def far_grad_kernel(res_ref, *refs):
    eff_refs, grad_ref = refs[:-1], refs[-1]
    deep = eff_refs[0].shape[0]
    for number, eff_ref in enumerate(eff_refs):
        grad = dot(res_ref[...], eff_ref[...], 1, 1)
        grad_ref[:, piece_columns(number, deep)] = grad.astype(BF16)


def head_kernel(width, x_ref, eff_ref, weight_ref, grad_ref, res_ref):
    predicted = dot(x_ref[:, :width], eff_ref[...])
    residual = (weight_ref[...] * (predicted - x_ref[:, width:].astype(F32))).astype(BF16)
    res_ref[...] = residual
    grad_ref[...] = dot(residual, eff_ref[...], 1, 1).astype(BF16)


def far_raw_kernel(x_ref, res_ref, out_ref):
    out_ref[...] = dot(x_ref[...], res_ref[...], 0, 0).astype(BF16)


def raw_kernel(first, x_ref, res_ref, far_ref, pattern_ref, before_ref, raw_ref, square_ref):
    step = pl.program_id(0)
    size, channels = raw_ref.shape
    raw = dot(x_ref[...], res_ref[...], 0, 0) + far_ref[...].astype(F32)

    @pl.when(step == 0)
    def _():
        square_ref[...] = before_ref[...]

    for i in range(size // BLK):
        for j in range(channels // BLK):
            rows, cols = slice(i * BLK, (i + 1) * BLK), slice(j * BLK, (j + 1) * BLK)
            used = pattern_ref[0, first + step * (size // BLK) + i, j].astype(F32)
            part = raw[rows, cols] * used
            raw_ref[rows, cols] = part
            square_ref[...] += jnp.sum((part * part).reshape(BLK // 8, 8, BLK), 0)


def scale_kernel(limit, parts, *refs):
    raw_refs, square_ref, out_ref = refs[:parts], refs[parts], refs[parts + 1]
    squares = jnp.sum(square_ref[...], keepdims=True)
    factor = jnp.minimum(1.0, limit / jnp.sqrt(squares + 1e-06))
    step = pl.program_id(0)
    per = pl.num_programs(0) // parts
    for part in range(parts):

        @pl.when(step // per == part)
        def _():
            out_ref[...] = (raw_refs[part][...] * factor)[None]


def far_place_kernel(back_ref, got_ref, out_ref):
    out_ref[...] = dot(back_ref[...], got_ref[...]).astype(BF16)


def place_back_kernel(back_ref, got_ref, far_ref, out_ref):
    out = dot(back_ref[...], got_ref[...]) + far_ref[...].astype(F32)
    out_ref[...] = out.astype(BF16)


def per_device(latents, obs_inst, owner_slot, head_weights, error_weight, block_pattern, targets):
    members, groups = lax.axis_size("loc"), lax.axis_size("grp")
    local_heads, width, channels = head_weights.shape
    heads = local_heads * members
    rows = latents.shape[0]
    capacity = 2 * rows // heads
    half = members // 2
    placed = half * capacity
    wide = width + channels
    inst = obs_inst.reshape(1, rows)
    halves = [list(range(half)), list(range(half, members))]

    def partner(x):
        return lax.ppermute(x, "loc", [(i, i ^ half) for i in range(members)])

    def hop(x, distance):
        return lax.ppermute(x, "loc", [(i, i ^ distance) for i in range(members)])

    def in_half(x):
        return lax.all_to_all(
            x, "loc", split_axis=0, concat_axis=0, tiled=True, axis_index_groups=halves
        )

    cut = 4

    def prep(near, name):
        return pl.pallas_call(
            functools.partial(prep_kernel, heads, capacity, near),
            grid=(cut,),
            in_specs=[whole((1, rows)), SMEM, whole((rows, width)), whole((rows, channels))],
            out_specs=pl.BlockSpec((placed // cut, wide), lambda i: (i, 0)),
            out_shape=jax.ShapeDtypeStruct((placed, wide), BF16),
            scratch_shapes=[pltpu.VMEM((8, rows), jnp.int32)],
            compiler_params=STREAM,
            cost_estimate=cost(2 * placed * rows * wide, 2 * (placed + rows) * wide),
            name=name,
        )(inst, owner_slot, latents, targets)

    far_send = prep(False, "prep_far")
    far_send = prep(False, "prep_far")
    near_send = prep(True, "prep_near")
    deep = width // (groups * CHUNKS)
    head_weights, far_send = lax.optimization_barrier((head_weights, far_send))
    pieces = pl.pallas_call(
        piece_kernel,
        in_specs=[VMEM, SMEM],
        out_specs=[VMEM] * CHUNKS,
        out_shape=[jax.ShapeDtypeStruct((deep, channels), BF16)] * CHUNKS,
        compiler_params=STREAM,
        cost_estimate=cost(CHUNKS * deep * channels, 4 * CHUNKS * deep * channels),
        name="piece",
    )(head_weights, block_pattern)
    far_weight = partner(error_weight)
    crossed = [partner(piece) for piece in pieces]
    crossed[0], near_send = lax.optimization_barrier((crossed[0], near_send))
    swapped = [[piece] for piece in crossed]
    step = 1
    while step < groups:
        swap = [(i, i ^ step) for i in range(groups)]
        swapped = [held + [lax.ppermute(x, "grp", swap) for x in held] for held in swapped]
        step *= 2
    far_eff = [swapped[chunk][number] for number in range(groups) for chunk in range(CHUNKS)]

    far_x = in_half(far_send)
    last = swapped[-1][groups // 2 :]
    swapped[-1] = swapped[-1][: groups // 2]
    near_send, far_x, swapped, far_weight = lax.optimization_barrier(
        (near_send, far_x, swapped, far_weight)
    )
    swapped[-1] = swapped[-1] + last
    far_eff = [swapped[chunk][number] for number in range(groups) for chunk in range(CHUNKS)]
    near_x = in_half(near_send)

    near_back, far_back = pl.pallas_call(
        functools.partial(back_kernel, heads, capacity),
        in_specs=[VMEM, SMEM],
        out_specs=[VMEM, VMEM],
        out_shape=[jax.ShapeDtypeStruct((rows, placed), BF16)] * 2,
        compiler_params=SMALL,
        cost_estimate=cost(2 * rows * rows * 128, 4 * rows * placed),
        name="back_places",
    )(inst, owner_slot)
    effective = pl.pallas_call(
        effective_kernel,
        in_specs=[VMEM, SMEM],
        out_specs=VMEM,
        out_shape=jax.ShapeDtypeStruct((width, channels), BF16),
        compiler_params=SMALL,
        cost_estimate=cost(width * channels, 4 * width * channels),
        name="effective",
    )(head_weights, block_pattern)
    far_x, effective, near_back, far_back = lax.optimization_barrier(
        (far_x, effective, near_back, far_back)
    )

    size = placed // 2
    row_spec = pl.BlockSpec((size, wide), lambda i: (i, 0))
    res_spec = pl.BlockSpec((size, channels), lambda i: (i, 0))
    far_specs = [whole((deep, channels))] * len(far_eff)
    far_res = pl.pallas_call(
        functools.partial(far_res_kernel, width),
        grid=(2,),
        in_specs=[row_spec, whole((1, channels))] + far_specs,
        out_specs=res_spec,
        out_shape=jax.ShapeDtypeStruct((placed, channels), BF16),
        compiler_params=SMALL,
        cost_estimate=cost(2 * placed * width * channels, 2 * placed * wide),
        name="far_res",
    )(far_x, far_weight, *far_eff)

    tall = 256
    steps = width // (CHUNKS * tall)
    far_raw = []
    for chunk in range(CHUNKS):
        part = pl.pallas_call(
            far_raw_kernel,
            grid=(steps,),
            in_specs=[
                pl.BlockSpec((placed, tall), lambda i, chunk=chunk: (0, chunk * steps + i)),
                whole((placed, channels)),
            ],
            out_specs=pl.BlockSpec((tall, channels), lambda i: (i, 0)),
            out_shape=jax.ShapeDtypeStruct((width // CHUNKS, channels), BF16),
            compiler_params=SMALL,
            cost_estimate=cost(2 * placed * width * channels // CHUNKS, 2 * width * channels),
            name="far_raw",
        )(far_x, far_res)
        far_raw.append(part)
    sent = far_raw
    far_raw = [partner(part) for part in sent]

    grad_spec = pl.BlockSpec((size, width), lambda i: (i, 0))
    far_grad = pl.pallas_call(
        far_grad_kernel,
        grid=(2,),
        in_specs=[res_spec] + far_specs,
        out_specs=grad_spec,
        out_shape=jax.ShapeDtypeStruct((placed, width), BF16),
        compiler_params=SMALL,
        cost_estimate=cost(2 * placed * width * channels, 2 * placed * wide),
        name="far_grad",
    )(far_res, *far_eff)
    far_grad, sent = lax.optimization_barrier((far_grad, sent))
    far_got = in_half(far_grad)
    near_grad, near_res = pl.pallas_call(
        functools.partial(head_kernel, width),
        grid=(2,),
        in_specs=[row_spec, whole((width, channels)), whole((1, channels))],
        out_specs=[grad_spec, res_spec],
        out_shape=[
            jax.ShapeDtypeStruct((placed, width), BF16),
            jax.ShapeDtypeStruct((placed, channels), BF16),
        ],
        compiler_params=SMALL,
        cost_estimate=cost(1 << 40, 1 << 30),
        name="near_head",
    )(near_x, effective, error_weight)
    near_grad, far_got = lax.optimization_barrier((near_grad, far_got))
    near_got = in_half(near_grad)

    def column_spec(deep):
        return pl.BlockSpec((deep, width // cut), lambda i: (0, i))

    far_placed = pl.pallas_call(
        far_place_kernel,
        grid=(cut,),
        in_specs=[whole((rows, placed)), column_spec(placed)],
        out_specs=column_spec(rows),
        out_shape=jax.ShapeDtypeStruct((rows, width), BF16),
        compiler_params=SMALL,
        cost_estimate=cost(2 * rows * placed * width, 4 * placed * width),
        name="far_place",
    )(far_back, far_got)
    far_raw[0], far_placed = lax.optimization_barrier((far_raw[0], far_placed))
    raw_grad, squares = [], jnp.zeros((8, 128), F32)
    for chunk in range(CHUNKS):
        part, squares = pl.pallas_call(
            functools.partial(raw_kernel, chunk * steps * (tall // BLK)),
            grid=(steps,),
            in_specs=[
                pl.BlockSpec((placed, tall), lambda i, chunk=chunk: (0, chunk * steps + i)),
                whole((placed, channels)),
                pl.BlockSpec((tall, channels), lambda i: (i, 0)),
                SMEM,
                whole((8, 128)),
            ],
            out_specs=[pl.BlockSpec((tall, channels), lambda i: (i, 0)), whole((8, 128))],
            out_shape=[
                jax.ShapeDtypeStruct((width // CHUNKS, channels), F32),
                jax.ShapeDtypeStruct((8, 128), F32),
            ],
            compiler_params=SMALL,
            cost_estimate=cost(1 << 40, 1 << 30),
            name="raw",
        )(near_x, near_res, far_raw[chunk], block_pattern, squares)
        raw_grad.append(part)
    step = 1
    while step < members:
        ways = min(4, members // step)
        squares = squares + sum(hop(squares, step * way) for way in range(1, ways))
        if step == 1:
            near_got, squares = lax.optimization_barrier((near_got, squares))
        step *= ways

    latent_grad = pl.pallas_call(
        place_back_kernel,
        grid=(cut,),
        in_specs=[whole((rows, placed)), column_spec(placed), column_spec(rows)],
        out_specs=column_spec(rows),
        out_shape=jax.ShapeDtypeStruct((rows, width), BF16),
        compiler_params=SMALL,
        cost_estimate=cost(2 * rows * placed * width, 4 * placed * width),
        name="place_back",
    )(near_back, near_got, far_placed)
    latent_grad, squares = lax.optimization_barrier((latent_grad, squares))
    def raw_spec(part):
        low = part * (cut // CHUNKS)
        return pl.BlockSpec(
            (width // cut, channels), lambda i: (jnp.clip(i - low, 0, cut // CHUNKS - 1), 0)
        )

    head_grad = pl.pallas_call(
        functools.partial(scale_kernel, math.sqrt(heads * width * channels), CHUNKS),
        grid=(cut,),
        in_specs=[raw_spec(part) for part in range(CHUNKS)] + [whole((8, 128))],
        out_specs=pl.BlockSpec((1, width // cut, channels), lambda i: (0, i, 0)),
        out_shape=jax.ShapeDtypeStruct((1, width, channels), F32),
        compiler_params=SMALL,
        cost_estimate=cost(width * channels, 8 * width * channels),
        name="scale",
    )(*raw_grad, squares)
    return (latent_grad, head_grad)


def solution(mesh):
    in_specs = (
        P(("grp", "loc"), None),
        P(("grp", "loc"), None),
        P(),
        P("loc", None, None),
        P("loc", None),
        P("loc", None, None),
        P(("grp", "loc"), None),
    )
    out_specs = (P(("grp", "loc"), None), P(("grp", "loc"), None, None))
    return jax.shard_map(
        per_device, mesh=mesh, in_specs=in_specs, out_specs=out_specs, check_vma=False
    )
```

```python
import functools
import math

import jax
import jax.numpy as jnp
from jax import lax
from jax.experimental import pallas as pl
from jax.experimental.pallas import tpu as pltpu
from jax.sharding import PartitionSpec as P


BLK = 128
TERMS = 16
CHUNKS = 4
PARTS = 2
F32 = jnp.float32
BF16 = jnp.bfloat16
VMEM = pl.BlockSpec(memory_space=pltpu.VMEM)
SMEM = pl.BlockSpec(memory_space=pltpu.SMEM)
STREAM = pltpu.CompilerParams(vmem_limit_bytes=60 * 1024 * 1024)
SMALL = pltpu.CompilerParams(vmem_limit_bytes=24 * 1024 * 1024)


def dot(a, b, ca=1, cb=0):
    return lax.dot_general(a, b, (((ca,), (cb,)), ((), ())), preferred_element_type=F32)


def cost(flops, nbytes):
    return pl.CostEstimate(flops=int(flops), bytes_accessed=int(nbytes), transcendentals=0)


def whole(shape):
    return pl.BlockSpec(shape, lambda i: (0,) * len(shape))


def places(inst, owner_ref, heads):
    rows = inst.shape[1]
    slot = jnp.zeros_like(inst)
    for k in range(heads):
        slot = jnp.where(inst == k, owner_ref[k], slot)
    hit = lax.broadcasted_iota(jnp.int32, (heads, rows), 0) == slot
    upto = lax.broadcasted_iota(jnp.int32, (rows, rows), 0) <= lax.broadcasted_iota(
        jnp.int32, (rows, rows), 1
    )
    count = dot(hit.astype(BF16), upto.astype(BF16))
    rank = jnp.sum(jnp.where(hit, count, 0.0), 0, keepdims=True).astype(jnp.int32) - 1
    return slot, rank


def half_places(inst, owner_ref, heads, capacity):
    slot, rank = places(inst, owner_ref, heads)
    half = heads // 2
    mine = (slot >= half) == (lax.axis_index("loc") >= half)
    head = jnp.where(slot >= half, slot - half, slot)
    return mine, jnp.where(mine, head, head ^ (half // 2)), rank


def one_hot_back(pos, size):
    column = jnp.transpose(jnp.broadcast_to(pos.astype(F32), (128, pos.shape[1])))[:, :1]
    number = lax.broadcasted_iota(jnp.int32, (pos.shape[1], size), 1)
    return (number == column.astype(jnp.int32)).astype(F32).astype(BF16)


def prep_kernel(heads, capacity, near, inst_ref, owner_ref, x_ref, t_ref, out_ref, place_ref):
    size, width = out_ref.shape[0], x_ref.shape[1]
    step = pl.program_id(0)

    @pl.when(step == 0)
    def _():
        mine, head, rank = half_places(inst_ref[...], owner_ref, heads, capacity)
        place = jnp.where(mine == near, head * capacity + rank, -1)
        place_ref[...] = jnp.broadcast_to(place, place_ref.shape)

    number = lax.broadcasted_iota(jnp.int32, (size, inst_ref.shape[1]), 0) + step * size
    pick = (number == place_ref[0:1, :]).astype(F32).astype(BF16)
    out_ref[:, :width] = dot(pick, x_ref[...]).astype(BF16)
    out_ref[:, width:] = dot(pick, t_ref[...]).astype(BF16)


def back_kernel(heads, capacity, inst_ref, owner_ref, near_ref, far_ref):
    mine, head, rank = half_places(inst_ref[...], owner_ref, heads, capacity)
    place = head * capacity + rank
    near_ref[...] = one_hot_back(jnp.where(mine, place, -1), near_ref.shape[1])
    far_ref[...] = one_hot_back(jnp.where(mine, -1, place), far_ref.shape[1])


def masked(block, pattern_ref, row, column):
    return (block.astype(F32) * pattern_ref[0, row, column].astype(F32)).astype(BF16)


def piece_kernel(w_ref, pattern_ref, weight_ref, *out_refs):
    rows, channels = out_refs[0].shape
    high = weight_ref[...].astype(BF16)
    rest = weight_ref[...] - high.astype(F32)
    middle = rest.astype(BF16)
    low = (rest - middle.astype(F32)).astype(BF16)
    line = lax.broadcasted_iota(jnp.int32, (TERMS, channels), 0)
    terms = jnp.where(line == 0, high.astype(F32), jnp.where(line == 1, middle.astype(F32), 0.0))
    out_refs[-1][rows:, :] = jnp.where(line == 2, low.astype(F32), terms).astype(BF16)
    for chunk, out_ref in enumerate(out_refs):
        first = (lax.axis_index("grp") * len(out_refs) + chunk) * (rows // BLK)
        for i in range(rows // BLK):
            here = pl.ds(pl.multiple_of((first + i) * BLK, BLK), BLK)
            for j in range(channels // BLK):
                cols = slice(j * BLK, (j + 1) * BLK)
                out_ref[i * BLK : (i + 1) * BLK, cols] = masked(
                    w_ref[0, here, cols], pattern_ref, first + i, j
                )


def effective_kernel(w_ref, pattern_ref, out_ref):
    width, channels = out_ref.shape
    for i in range(width // BLK):
        for j in range(channels // BLK):
            rows, cols = slice(i * BLK, (i + 1) * BLK), slice(j * BLK, (j + 1) * BLK)
            out_ref[rows, cols] = masked(w_ref[0, rows, cols], pattern_ref, i, j)


def piece_columns(number, deep):
    first = (lax.axis_index("grp") ^ (number // CHUNKS)) * CHUNKS + number % CHUNKS
    return pl.ds(pl.multiple_of(first * deep, deep), deep)


def far_res_kernel(width, x_ref, *refs):
    eff_refs, res_ref = refs[:-1], refs[-1]
    deep = eff_refs[0].shape[0]
    predicted = dot(x_ref[:, piece_columns(0, deep)], eff_refs[0][:deep])
    for number in range(1, len(eff_refs)):
        predicted += dot(x_ref[:, piece_columns(number, deep)], eff_refs[number][:deep])
    misfit = predicted - x_ref[:, width:].astype(F32)
    terms = eff_refs[CHUNKS - 1][deep:].astype(F32)
    weight = terms[0:1] + terms[1:2] + terms[2:3]
    res_ref[...] = (weight * misfit).astype(BF16)


def far_grad_kernel(res_ref, *refs):
    eff_refs, grad_ref = refs[:-1], refs[-1]
    deep = eff_refs[0].shape[0]
    for number, eff_ref in enumerate(eff_refs):
        grad = dot(res_ref[...], eff_ref[:deep], 1, 1)
        grad_ref[:, piece_columns(number, deep)] = grad.astype(BF16)


def head_kernel(width, x_ref, eff_ref, weight_ref, grad_ref, res_ref):
    predicted = dot(x_ref[:, :width], eff_ref[...])
    residual = (weight_ref[...] * (predicted - x_ref[:, width:].astype(F32))).astype(BF16)
    res_ref[...] = residual
    grad_ref[...] = dot(residual, eff_ref[...], 1, 1).astype(BF16)


def far_raw_kernel(x_ref, res_ref, out_ref):
    out_ref[...] = dot(x_ref[...], res_ref[...], 0, 0).astype(BF16)


def raw_kernel(first, x_ref, res_ref, far_ref, out_ref, pattern_ref, before_ref, raw_ref, square_ref):
    step = pl.program_id(0)
    size, channels = raw_ref.shape
    raw = dot(x_ref[...], res_ref[...], 0, 0) + far_ref[...].astype(F32)
    raw = raw + out_ref[...].astype(F32)

    @pl.when(step == 0)
    def _():
        square_ref[...] = before_ref[...]

    for i in range(size // BLK):
        for j in range(channels // BLK):
            rows, cols = slice(i * BLK, (i + 1) * BLK), slice(j * BLK, (j + 1) * BLK)
            used = pattern_ref[0, first + step * (size // BLK) + i, j].astype(F32)
            part = raw[rows, cols] * used
            raw_ref[rows, cols] = part
            square_ref[...] += jnp.sum((part * part).reshape(BLK // 8, 8, BLK), 0)


def far_place_kernel(back_ref, got_ref, out_ref):
    out_ref[...] = dot(back_ref[...], got_ref[...]).astype(BF16)


def finish_kernel(limit, parts, back_ref, got_ref, far_ref, square_ref, *refs):
    raw_refs, (out_ref, head_ref) = refs[:parts], refs[parts:]
    squares = jnp.sum(square_ref[...], keepdims=True)
    factor = jnp.minimum(1.0, limit / jnp.sqrt(squares + 1e-06))
    step = pl.program_id(0)
    per = pl.num_programs(0) // parts
    for part in range(parts):

        @pl.when(step // per == part)
        def _():
            head_ref[...] = (raw_refs[part][...] * factor)[None]

    out = dot(back_ref[...], got_ref[...]) + far_ref[...].astype(F32)
    out_ref[...] = out.astype(BF16)


def per_device(latents, obs_inst, owner_slot, head_weights, error_weight, block_pattern, targets):
    members, groups = lax.axis_size("loc"), lax.axis_size("grp")
    local_heads, width, channels = head_weights.shape
    heads = local_heads * members
    rows = latents.shape[0]
    capacity = 2 * rows // heads
    half = members // 2
    placed = half * capacity
    apart = half + half // 2
    wide = width + channels
    inst = obs_inst.reshape(1, rows)
    halves = [list(range(half)), list(range(half, members))]

    def partner(x):
        return lax.ppermute(x, "loc", [(i, i ^ apart) for i in range(members)])

    def hop(x, distance):
        return lax.ppermute(x, "loc", [(i, i ^ distance) for i in range(members)])

    def in_half(x):
        return lax.all_to_all(
            x, "loc", split_axis=0, concat_axis=0, tiled=True, axis_index_groups=halves
        )

    cut = 4

    def prep(near, name):
        return pl.pallas_call(
            functools.partial(prep_kernel, heads, capacity, near),
            grid=(cut,),
            in_specs=[whole((1, rows)), SMEM, whole((rows, width)), whole((rows, channels))],
            out_specs=pl.BlockSpec((placed // cut, wide), lambda i: (i, 0)),
            out_shape=jax.ShapeDtypeStruct((placed, wide), BF16),
            scratch_shapes=[pltpu.VMEM((8, rows), jnp.int32)],
            compiler_params=STREAM,
            cost_estimate=cost(2 * placed * rows * wide, 2 * (placed + rows) * wide),
            name=name,
        )(inst, owner_slot, latents, targets)

    far_send = prep(False, "prep_far")
    far_send = prep(False, "prep_far")
    near_send = prep(True, "prep_near")
    deep = width // (groups * CHUNKS)
    head_weights, far_send = lax.optimization_barrier((head_weights, far_send))
    pieces = pl.pallas_call(
        piece_kernel,
        in_specs=[VMEM, SMEM, VMEM],
        out_specs=[VMEM] * CHUNKS,
        out_shape=[
            jax.ShapeDtypeStruct((deep + (TERMS if last else 0), channels), BF16)
            for last in [False] * (CHUNKS - 1) + [True]
        ],
        compiler_params=STREAM,
        cost_estimate=cost(CHUNKS * deep * channels, 4 * CHUNKS * deep * channels),
        name="piece",
    )(head_weights, block_pattern, error_weight)
    crossed = [partner(piece) for piece in pieces]
    crossed[0], near_send = lax.optimization_barrier((crossed[0], near_send))
    swapped = [[piece] for piece in crossed]
    step = 1
    while step < groups:
        swap = [(i, i ^ step) for i in range(groups)]
        swapped = [held + [lax.ppermute(x, "grp", swap) for x in held] for held in swapped]
        step *= 2
    far_eff = [swapped[chunk][number] for number in range(groups) for chunk in range(CHUNKS)]

    far_x = in_half(far_send)
    early = swapped[: CHUNKS // 4]
    near_send, far_x, early, crossed = lax.optimization_barrier((near_send, far_x, early, crossed))
    swapped[: CHUNKS // 4] = early
    far_eff = [swapped[chunk][number] for number in range(groups) for chunk in range(CHUNKS)]
    near_x = in_half(near_send)

    near_back, far_back = pl.pallas_call(
        functools.partial(back_kernel, heads, capacity),
        in_specs=[VMEM, SMEM],
        out_specs=[VMEM, VMEM],
        out_shape=[jax.ShapeDtypeStruct((rows, placed), BF16)] * 2,
        compiler_params=SMALL,
        cost_estimate=cost(2 * rows * rows * 128, 4 * rows * placed),
        name="back_places",
    )(inst, owner_slot)
    effective = pl.pallas_call(
        effective_kernel,
        in_specs=[VMEM, SMEM],
        out_specs=VMEM,
        out_shape=jax.ShapeDtypeStruct((width, channels), BF16),
        compiler_params=SMALL,
        cost_estimate=cost(width * channels, 4 * width * channels),
        name="effective",
    )(head_weights, block_pattern)
    far_x, effective, near_back, far_back = lax.optimization_barrier(
        (far_x, effective, near_back, far_back)
    )

    size = placed // 2
    row_spec = pl.BlockSpec((size, wide), lambda i: (i, 0))
    res_spec = pl.BlockSpec((size, channels), lambda i: (i, 0))
    far_specs = [whole(piece.shape) for piece in far_eff]
    far_res = pl.pallas_call(
        functools.partial(far_res_kernel, width),
        grid=(2,),
        in_specs=[row_spec] + far_specs,
        out_specs=res_spec,
        out_shape=jax.ShapeDtypeStruct((placed, channels), BF16),
        compiler_params=SMALL,
        cost_estimate=cost(2 * placed * width * channels, 2 * placed * wide),
        name="far_res",
    )(far_x, *far_eff)

    tall = 256
    steps = width // (PARTS * tall)
    far_raw = []
    for chunk in range(PARTS):
        part = pl.pallas_call(
            far_raw_kernel,
            grid=(steps,),
            in_specs=[
                pl.BlockSpec((placed, tall), lambda i, chunk=chunk: (0, chunk * steps + i)),
                whole((placed, channels)),
            ],
            out_specs=pl.BlockSpec((tall, channels), lambda i: (i, 0)),
            out_shape=jax.ShapeDtypeStruct((width // PARTS, channels), BF16),
            compiler_params=SMALL,
            cost_estimate=cost(2 * placed * width * channels // PARTS, 2 * width * channels),
            name="far_raw",
        )(far_x, far_res)
        far_raw.append(part)
    sent = far_raw
    bit = half // 2
    inner = [i for i in range(members) if (i // bit) % 2 != (i // half) % 2]
    outer = [i for i in range(members) if i not in inner]
    far_raw = [lax.ppermute(part, "loc", [(i, i ^ apart) for i in inner]) for part in sent]
    near_x, held = lax.optimization_barrier((near_x, sent))
    far_out = [lax.ppermute(part, "loc", [(i, i ^ apart) for i in outer]) for part in held]

    grad_spec = pl.BlockSpec((size, width), lambda i: (i, 0))
    far_grad = pl.pallas_call(
        far_grad_kernel,
        grid=(2,),
        in_specs=[res_spec] + far_specs,
        out_specs=grad_spec,
        out_shape=jax.ShapeDtypeStruct((placed, width), BF16),
        compiler_params=SMALL,
        cost_estimate=cost(2 * placed * width * channels, 2 * placed * wide),
        name="far_grad",
    )(far_res, *far_eff)
    far_grad, sent = lax.optimization_barrier((far_grad, sent))
    far_got = in_half(far_grad)
    near_grad, near_res = pl.pallas_call(
        functools.partial(head_kernel, width),
        grid=(2,),
        in_specs=[row_spec, whole((width, channels)), whole((1, channels))],
        out_specs=[grad_spec, res_spec],
        out_shape=[
            jax.ShapeDtypeStruct((placed, width), BF16),
            jax.ShapeDtypeStruct((placed, channels), BF16),
        ],
        compiler_params=SMALL,
        cost_estimate=cost(1 << 40, 1 << 30),
        name="near_head",
    )(near_x, effective, error_weight)
    near_grad, far_got = lax.optimization_barrier((near_grad, far_got))

    def column_spec(deep):
        return pl.BlockSpec((deep, width // cut), lambda i: (0, i))

    far_placed = pl.pallas_call(
        far_place_kernel,
        grid=(cut,),
        in_specs=[whole((rows, placed)), column_spec(placed)],
        out_specs=column_spec(rows),
        out_shape=jax.ShapeDtypeStruct((rows, width), BF16),
        compiler_params=SMALL,
        cost_estimate=cost(2 * rows * placed * width, 4 * placed * width),
        name="far_place",
    )(far_back, far_got)
    near_grad, far_placed = lax.optimization_barrier((near_grad, far_placed))
    near_got = in_half(near_grad)
    raw_grad, squares = [], jnp.zeros((8, 128), F32)
    for chunk in range(PARTS):
        part, squares = pl.pallas_call(
            functools.partial(raw_kernel, chunk * steps * (tall // BLK)),
            grid=(steps,),
            in_specs=[
                pl.BlockSpec((placed, tall), lambda i, chunk=chunk: (0, chunk * steps + i)),
                whole((placed, channels)),
                pl.BlockSpec((tall, channels), lambda i: (i, 0)),
                pl.BlockSpec((tall, channels), lambda i: (i, 0)),
                SMEM,
                whole((8, 128)),
            ],
            out_specs=[pl.BlockSpec((tall, channels), lambda i: (i, 0)), whole((8, 128))],
            out_shape=[
                jax.ShapeDtypeStruct((width // PARTS, channels), F32),
                jax.ShapeDtypeStruct((8, 128), F32),
            ],
            compiler_params=SMALL,
            cost_estimate=cost(1 << 40, 1 << 30),
            name="raw",
        )(near_x, near_res, far_raw[chunk], far_out[chunk], block_pattern, squares)
        raw_grad.append(part)
    step = 1
    while step < members:
        ways = min(4, members // step)
        squares = squares + sum(hop(squares, step * way) for way in range(1, ways))
        step *= ways

    near_got, squares = lax.optimization_barrier((near_got, squares))

    def raw_spec(part):
        low = part * (cut // PARTS)
        return pl.BlockSpec(
            (width // cut, channels), lambda i: (jnp.clip(i - low, 0, cut // PARTS - 1), 0)
        )

    latent_grad, head_grad = pl.pallas_call(
        functools.partial(finish_kernel, math.sqrt(heads * width * channels), PARTS),
        grid=(cut,),
        in_specs=[whole((rows, placed)), column_spec(placed), column_spec(rows), whole((8, 128))]
        + [raw_spec(part) for part in range(PARTS)],
        out_specs=[
            column_spec(rows),
            pl.BlockSpec((1, width // cut, channels), lambda i: (0, i, 0)),
        ],
        out_shape=[
            jax.ShapeDtypeStruct((rows, width), BF16),
            jax.ShapeDtypeStruct((1, width, channels), F32),
        ],
        compiler_params=STREAM,
        cost_estimate=cost(2 * rows * placed * width, 8 * width * channels),
        name="finish",
    )(near_back, near_got, far_placed, squares, *raw_grad)
    return (latent_grad, head_grad)


def solution(mesh):
    in_specs = (
        P(("grp", "loc"), None),
        P(("grp", "loc"), None),
        P(),
        P("loc", None, None),
        P("loc", None),
        P("loc", None, None),
        P(("grp", "loc"), None),
    )
    out_specs = (P(("grp", "loc"), None), P(("grp", "loc"), None, None))
    return jax.shard_map(
        per_device, mesh=mesh, in_specs=in_specs, out_specs=out_specs, check_vma=False
    )
```

```python
import functools
import math

import jax
import jax.numpy as jnp
from jax import lax
from jax.experimental import pallas as pl
from jax.experimental.pallas import tpu as pltpu
from jax.sharding import PartitionSpec as P


BLK = 128
TERMS = 16
CHUNKS = 4
PARTS = 2
F32 = jnp.float32
BF16 = jnp.bfloat16
VMEM = pl.BlockSpec(memory_space=pltpu.VMEM)
SMEM = pl.BlockSpec(memory_space=pltpu.SMEM)
STREAM = pltpu.CompilerParams(vmem_limit_bytes=60 * 1024 * 1024)
SMALL = pltpu.CompilerParams(vmem_limit_bytes=24 * 1024 * 1024)


def dot(a, b, ca=1, cb=0):
    return lax.dot_general(a, b, (((ca,), (cb,)), ((), ())), preferred_element_type=F32)


def cost(flops, nbytes):
    return pl.CostEstimate(flops=int(flops), bytes_accessed=int(nbytes), transcendentals=0)


LATE = cost(1 << 40, 1 << 30)


def whole(shape):
    return pl.BlockSpec(shape, lambda i: (0,) * len(shape))


def places(inst, owner_ref, heads):
    rows = inst.shape[1]
    slot = jnp.zeros_like(inst)
    for k in range(heads):
        slot = jnp.where(inst == k, owner_ref[k], slot)
    hit = lax.broadcasted_iota(jnp.int32, (heads, rows), 0) == slot
    upto = lax.broadcasted_iota(jnp.int32, (rows, rows), 0) <= lax.broadcasted_iota(
        jnp.int32, (rows, rows), 1
    )
    count = dot(hit.astype(BF16), upto.astype(BF16))
    rank = jnp.sum(jnp.where(hit, count, 0.0), 0, keepdims=True).astype(jnp.int32) - 1
    return slot, rank


def half_places(inst, owner_ref, heads, capacity):
    slot, rank = places(inst, owner_ref, heads)
    half = heads // 2
    mine = (slot >= half) == (lax.axis_index("loc") >= half)
    head = jnp.where(slot >= half, slot - half, slot)
    return mine, jnp.where(mine, head, head ^ (half // 2)), rank


def one_hot_back(pos, size):
    column = jnp.transpose(jnp.broadcast_to(pos.astype(F32), (128, pos.shape[1])))[:, :1]
    number = lax.broadcasted_iota(jnp.int32, (pos.shape[1], size), 1)
    return (number == column.astype(jnp.int32)).astype(F32).astype(BF16)


def prep_kernel(heads, capacity, near, inst_ref, owner_ref, x_ref, t_ref, out_ref, place_ref):
    size, width = out_ref.shape[0], x_ref.shape[1]
    step = pl.program_id(0)

    @pl.when(step == 0)
    def _():
        mine, head, rank = half_places(inst_ref[...], owner_ref, heads, capacity)
        place = jnp.where(mine == near, head * capacity + rank, -1)
        place_ref[...] = jnp.broadcast_to(place, place_ref.shape)

    number = lax.broadcasted_iota(jnp.int32, (size, inst_ref.shape[1]), 0) + step * size
    pick = (number == place_ref[0:1, :]).astype(F32).astype(BF16)
    out_ref[:, :width] = dot(pick, x_ref[...]).astype(BF16)
    out_ref[:, width:] = dot(pick, t_ref[...]).astype(BF16)


def back_kernel(heads, capacity, inst_ref, owner_ref, near_ref, far_ref):
    mine, head, rank = half_places(inst_ref[...], owner_ref, heads, capacity)
    place = head * capacity + rank
    near_ref[...] = one_hot_back(jnp.where(mine, place, -1), near_ref.shape[1])
    far_ref[...] = one_hot_back(jnp.where(mine, -1, place), far_ref.shape[1])


def masked(block, pattern_ref, row, column):
    return (block.astype(F32) * pattern_ref[0, row, column].astype(F32)).astype(BF16)


def piece_kernel(w_ref, pattern_ref, weight_ref, *out_refs):
    rows, channels = out_refs[0].shape
    high = weight_ref[...].astype(BF16)
    rest = weight_ref[...] - high.astype(F32)
    middle = rest.astype(BF16)
    low = (rest - middle.astype(F32)).astype(BF16)
    line = lax.broadcasted_iota(jnp.int32, (TERMS, channels), 0)
    terms = jnp.where(line == 0, high.astype(F32), jnp.where(line == 1, middle.astype(F32), 0.0))
    out_refs[-1][rows:, :] = jnp.where(line == 2, low.astype(F32), terms).astype(BF16)
    for chunk, out_ref in enumerate(out_refs):
        first = (lax.axis_index("grp") * len(out_refs) + chunk) * (rows // BLK)
        for i in range(rows // BLK):
            here = pl.ds(pl.multiple_of((first + i) * BLK, BLK), BLK)
            for j in range(channels // BLK):
                cols = slice(j * BLK, (j + 1) * BLK)
                out_ref[i * BLK : (i + 1) * BLK, cols] = masked(
                    w_ref[0, here, cols], pattern_ref, first + i, j
                )


def effective_kernel(w_ref, pattern_ref, out_ref):
    width, channels = out_ref.shape
    for i in range(width // BLK):
        for j in range(channels // BLK):
            rows, cols = slice(i * BLK, (i + 1) * BLK), slice(j * BLK, (j + 1) * BLK)
            out_ref[rows, cols] = masked(w_ref[0, rows, cols], pattern_ref, i, j)


def piece_columns(number, deep):
    first = (lax.axis_index("grp") ^ (number // CHUNKS)) * CHUNKS + number % CHUNKS
    return pl.ds(pl.multiple_of(first * deep, deep), deep)


def far_res_kernel(width, x_ref, *refs):
    eff_refs, res_ref = refs[:-1], refs[-1]
    deep = eff_refs[0].shape[0]
    predicted = dot(x_ref[:, piece_columns(0, deep)], eff_refs[0][:deep])
    for number in range(1, len(eff_refs)):
        predicted += dot(x_ref[:, piece_columns(number, deep)], eff_refs[number][:deep])
    misfit = predicted - x_ref[:, width:].astype(F32)
    terms = eff_refs[CHUNKS - 1][deep:].astype(F32)
    weight = terms[0:1] + terms[1:2] + terms[2:3]
    res_ref[...] = (weight * misfit).astype(BF16)


def far_grad_kernel(res_ref, *refs):
    eff_refs, grad_ref = refs[:-1], refs[-1]
    deep = eff_refs[0].shape[0]
    for number, eff_ref in enumerate(eff_refs):
        grad = dot(res_ref[...], eff_ref[:deep], 1, 1)
        grad_ref[:, piece_columns(number, deep)] = grad.astype(BF16)


def head_kernel(width, x_ref, eff_ref, weight_ref, grad_ref, res_ref):
    predicted = dot(x_ref[:, :width], eff_ref[...])
    residual = (weight_ref[...] * (predicted - x_ref[:, width:].astype(F32))).astype(BF16)
    res_ref[...] = residual
    grad_ref[...] = dot(residual, eff_ref[...], 1, 1).astype(BF16)


def far_raw_kernel(x_ref, res_ref, out_ref):
    out_ref[...] = dot(x_ref[...], res_ref[...], 0, 0).astype(BF16)


def raw_kernel(first, x_ref, res_ref, far_ref, out_ref, pattern_ref, before_ref, raw_ref, square_ref):
    step = pl.program_id(0)
    size, channels = raw_ref.shape
    raw = dot(x_ref[...], res_ref[...], 0, 0) + far_ref[...].astype(F32)
    raw = raw + out_ref[...].astype(F32)

    @pl.when(step == 0)
    def _():
        square_ref[...] = before_ref[...]

    for i in range(size // BLK):
        for j in range(channels // BLK):
            rows, cols = slice(i * BLK, (i + 1) * BLK), slice(j * BLK, (j + 1) * BLK)
            used = pattern_ref[0, first + step * (size // BLK) + i, j].astype(F32)
            part = raw[rows, cols] * used
            raw_ref[rows, cols] = part
            square_ref[...] += jnp.sum((part * part).reshape(BLK // 8, 8, BLK), 0)


def far_place_kernel(back_ref, got_ref, out_ref):
    out_ref[...] = dot(back_ref[...], got_ref[...]).astype(BF16)


def finish_kernel(limit, parts, back_ref, got_ref, far_ref, square_ref, *refs):
    raw_refs, (out_ref, head_ref) = refs[:parts], refs[parts:]
    squares = jnp.sum(square_ref[...], keepdims=True)
    factor = jnp.minimum(1.0, limit / jnp.sqrt(squares + 1e-06))
    step = pl.program_id(0)
    per = pl.num_programs(0) // parts
    for part in range(parts):

        @pl.when(step // per == part)
        def _():
            head_ref[...] = (raw_refs[part][...] * factor)[None]

    out = dot(back_ref[...], got_ref[...]) + far_ref[...].astype(F32)
    out_ref[...] = out.astype(BF16)


def per_device(latents, obs_inst, owner_slot, head_weights, error_weight, block_pattern, targets):
    members, groups = lax.axis_size("loc"), lax.axis_size("grp")
    local_heads, width, channels = head_weights.shape
    heads = local_heads * members
    rows = latents.shape[0]
    capacity = 2 * rows // heads
    half = members // 2
    placed = half * capacity
    apart = half + half // 2
    wide = width + channels
    inst = obs_inst.reshape(1, rows)
    halves = [list(range(half)), list(range(half, members))]

    def partner(x):
        return lax.ppermute(x, "loc", [(i, i ^ apart) for i in range(members)])

    def hop(x, distance):
        return lax.ppermute(x, "loc", [(i, i ^ distance) for i in range(members)])

    def in_half(x):
        return lax.all_to_all(
            x, "loc", split_axis=0, concat_axis=0, tiled=True, axis_index_groups=halves
        )

    cut = 4

    def prep(near, name):
        return pl.pallas_call(
            functools.partial(prep_kernel, heads, capacity, near),
            grid=(2,),
            in_specs=[whole((1, rows)), SMEM, whole((rows, width)), whole((rows, channels))],
            out_specs=pl.BlockSpec((placed // 2, wide), lambda i: (i, 0)),
            out_shape=jax.ShapeDtypeStruct((placed, wide), BF16),
            scratch_shapes=[pltpu.VMEM((8, rows), jnp.int32)],
            compiler_params=STREAM,
            cost_estimate=cost(2 * placed * rows * wide, 2 * (placed + rows) * wide),
            name=name,
        )(inst, owner_slot, latents, targets)

    far_send = prep(False, "prep_far")
    near_send = prep(True, "prep_near")
    deep = width // (groups * CHUNKS)
    head_weights, far_send = lax.optimization_barrier((head_weights, far_send))
    pieces = pl.pallas_call(
        piece_kernel,
        in_specs=[VMEM, SMEM, VMEM],
        out_specs=[VMEM] * CHUNKS,
        out_shape=[
            jax.ShapeDtypeStruct((deep + (TERMS if last else 0), channels), BF16)
            for last in [False] * (CHUNKS - 1) + [True]
        ],
        compiler_params=STREAM,
        cost_estimate=cost(CHUNKS * deep * channels, 4 * CHUNKS * deep * channels),
        name="piece",
    )(head_weights, block_pattern, error_weight)
    crossed = [partner(piece) for piece in pieces]
    crossed[0], near_send = lax.optimization_barrier((crossed[0], near_send))
    swapped = [[piece] for piece in crossed]
    step = 1
    while step < groups:
        swap = [(i, i ^ step) for i in range(groups)]
        swapped = [held + [lax.ppermute(x, "grp", swap) for x in held] for held in swapped]
        step *= 2
    far_x = in_half(far_send)
    early = swapped[: CHUNKS // 4]
    near_send, far_x, early, crossed = lax.optimization_barrier((near_send, far_x, early, crossed))
    swapped[: CHUNKS // 4] = early
    far_eff = [swapped[chunk][number] for number in range(groups) for chunk in range(CHUNKS)]
    near_x = in_half(near_send)

    near_back, far_back = pl.pallas_call(
        functools.partial(back_kernel, heads, capacity),
        in_specs=[VMEM, SMEM],
        out_specs=[VMEM, VMEM],
        out_shape=[jax.ShapeDtypeStruct((rows, placed), BF16)] * 2,
        compiler_params=SMALL,
        cost_estimate=cost(2 * rows * rows * 128, 4 * rows * placed),
        name="back_places",
    )(inst, owner_slot)
    effective = pl.pallas_call(
        effective_kernel,
        in_specs=[VMEM, SMEM],
        out_specs=VMEM,
        out_shape=jax.ShapeDtypeStruct((width, channels), BF16),
        compiler_params=SMALL,
        cost_estimate=cost(width * channels, 4 * width * channels),
        name="effective",
    )(head_weights, block_pattern)
    far_x, effective, near_back, far_back = lax.optimization_barrier(
        (far_x, effective, near_back, far_back)
    )

    size = placed // 2
    row_spec = pl.BlockSpec((size, wide), lambda i: (i, 0))
    res_spec = pl.BlockSpec((size, channels), lambda i: (i, 0))
    far_specs = [whole(piece.shape) for piece in far_eff]
    far_res = pl.pallas_call(
        functools.partial(far_res_kernel, width),
        grid=(2,),
        in_specs=[row_spec] + far_specs,
        out_specs=res_spec,
        out_shape=jax.ShapeDtypeStruct((placed, channels), BF16),
        compiler_params=SMALL,
        cost_estimate=cost(2 * placed * width * channels, 2 * placed * wide),
        name="far_res",
    )(far_x, *far_eff)

    tall = 256
    steps = width // (PARTS * tall)
    far_raw = []
    for chunk in range(PARTS):
        part = pl.pallas_call(
            far_raw_kernel,
            grid=(steps,),
            in_specs=[
                pl.BlockSpec((placed, tall), lambda i, chunk=chunk: (0, chunk * steps + i)),
                whole((placed, channels)),
            ],
            out_specs=pl.BlockSpec((tall, channels), lambda i: (i, 0)),
            out_shape=jax.ShapeDtypeStruct((width // PARTS, channels), BF16),
            compiler_params=SMALL,
            cost_estimate=cost(2 * placed * width * channels // PARTS, 2 * width * channels),
            name="far_raw",
        )(far_x, far_res)
        far_raw.append(part)
    sent = far_raw
    bit = half // 2
    inner = [i for i in range(members) if (i // bit) % 2 != (i // half) % 2]
    outer = [i for i in range(members) if i not in inner]
    far_raw = [lax.ppermute(part, "loc", [(i, i ^ apart) for i in inner]) for part in sent]
    near_x, held = lax.optimization_barrier((near_x, sent))
    far_out = [lax.ppermute(part, "loc", [(i, i ^ apart) for i in outer]) for part in held]

    grad_spec = pl.BlockSpec((size, width), lambda i: (i, 0))
    far_grad = pl.pallas_call(
        far_grad_kernel,
        grid=(2,),
        in_specs=[res_spec] + far_specs,
        out_specs=grad_spec,
        out_shape=jax.ShapeDtypeStruct((placed, width), BF16),
        compiler_params=SMALL,
        cost_estimate=cost(2 * placed * width * channels, 2 * placed * wide),
        name="far_grad",
    )(far_res, *far_eff)
    far_grad, sent = lax.optimization_barrier((far_grad, sent))
    far_got = in_half(far_grad)
    near_grad, near_res = pl.pallas_call(
        functools.partial(head_kernel, width),
        grid=(2,),
        in_specs=[row_spec, whole((width, channels)), whole((1, channels))],
        out_specs=[grad_spec, res_spec],
        out_shape=[
            jax.ShapeDtypeStruct((placed, width), BF16),
            jax.ShapeDtypeStruct((placed, channels), BF16),
        ],
        compiler_params=SMALL,
        cost_estimate=LATE,
        name="near_head",
    )(near_x, effective, error_weight)
    near_grad, far_got = lax.optimization_barrier((near_grad, far_got))

    def column_spec(deep):
        return pl.BlockSpec((deep, width // cut), lambda i: (0, i))

    def half_spec(deep):
        return pl.BlockSpec((deep, width // 2), lambda i: (0, i))

    far_placed = pl.pallas_call(
        far_place_kernel,
        grid=(2,),
        in_specs=[whole((rows, placed)), half_spec(placed)],
        out_specs=half_spec(rows),
        out_shape=jax.ShapeDtypeStruct((rows, width), BF16),
        compiler_params=STREAM,
        cost_estimate=cost(2 * rows * placed * width, 4 * placed * width),
        name="far_place",
    )(far_back, far_got)
    near_grad, far_placed = lax.optimization_barrier((near_grad, far_placed))
    near_got = in_half(near_grad)
    raw_grad, squares = [], jnp.zeros((8, 128), F32)
    for chunk in range(PARTS):
        part, squares = pl.pallas_call(
            functools.partial(raw_kernel, chunk * steps * (tall // BLK)),
            grid=(steps,),
            in_specs=[
                pl.BlockSpec((placed, tall), lambda i, chunk=chunk: (0, chunk * steps + i)),
                whole((placed, channels)),
                pl.BlockSpec((tall, channels), lambda i: (i, 0)),
                pl.BlockSpec((tall, channels), lambda i: (i, 0)),
                SMEM,
                whole((8, 128)),
            ],
            out_specs=[pl.BlockSpec((tall, channels), lambda i: (i, 0)), whole((8, 128))],
            out_shape=[
                jax.ShapeDtypeStruct((width // PARTS, channels), F32),
                jax.ShapeDtypeStruct((8, 128), F32),
            ],
            compiler_params=SMALL,
            cost_estimate=LATE,
            name="raw",
        )(near_x, near_res, far_raw[chunk], far_out[chunk], block_pattern, squares)
        raw_grad.append(part)
    step = 1
    while step < members:
        ways = min(4, members // step)
        squares = squares + sum(hop(squares, step * way) for way in range(1, ways))
        step *= ways

    near_got, squares = lax.optimization_barrier((near_got, squares))

    def raw_spec(part):
        low = part * (cut // PARTS)
        return pl.BlockSpec(
            (width // cut, channels), lambda i: (jnp.clip(i - low, 0, cut // PARTS - 1), 0)
        )

    latent_grad, head_grad = pl.pallas_call(
        functools.partial(finish_kernel, math.sqrt(heads * width * channels), PARTS),
        grid=(cut,),
        in_specs=[whole((rows, placed)), column_spec(placed), column_spec(rows), whole((8, 128))]
        + [raw_spec(part) for part in range(PARTS)],
        out_specs=[
            column_spec(rows),
            pl.BlockSpec((1, width // cut, channels), lambda i: (0, i, 0)),
        ],
        out_shape=[
            jax.ShapeDtypeStruct((rows, width), BF16),
            jax.ShapeDtypeStruct((1, width, channels), F32),
        ],
        compiler_params=STREAM,
        cost_estimate=cost(2 * rows * placed * width, 8 * width * channels),
        name="finish",
    )(near_back, near_got, far_placed, squares, *raw_grad)
    return (latent_grad, head_grad)


def solution(mesh):
    in_specs = (
        P(("grp", "loc"), None),
        P(("grp", "loc"), None),
        P(),
        P("loc", None, None),
        P("loc", None),
        P("loc", None, None),
        P(("grp", "loc"), None),
    )
    out_specs = (P(("grp", "loc"), None), P(("grp", "loc"), None, None))
    return jax.shard_map(
        per_device, mesh=mesh, in_specs=in_specs, out_specs=out_specs, check_vma=False
    )
```

```python
import functools
import math

import jax
import jax.numpy as jnp
from jax import lax
from jax.experimental import pallas as pl
from jax.experimental.pallas import tpu as pltpu
from jax.sharding import PartitionSpec as P


BLK = 128
TERMS = 16
CHUNKS = 4
PARTS = 2
F32 = jnp.float32
BF16 = jnp.bfloat16
VMEM = pl.BlockSpec(memory_space=pltpu.VMEM)
SMEM = pl.BlockSpec(memory_space=pltpu.SMEM)
STREAM = pltpu.CompilerParams(vmem_limit_bytes=60 * 1024 * 1024)
SMALL = pltpu.CompilerParams(vmem_limit_bytes=24 * 1024 * 1024)


def dot(a, b, ca=1, cb=0):
    return lax.dot_general(a, b, (((ca,), (cb,)), ((), ())), preferred_element_type=F32)


def cost(flops, nbytes):
    return pl.CostEstimate(flops=int(flops), bytes_accessed=int(nbytes), transcendentals=0)


LATE = cost(1 << 40, 1 << 30)


def whole(shape):
    return pl.BlockSpec(shape, lambda i: (0,) * len(shape))


def places(inst, owner_ref, heads):
    rows = inst.shape[1]
    slot = jnp.zeros_like(inst)
    for k in range(heads):
        slot = jnp.where(inst == k, owner_ref[k], slot)
    hit = lax.broadcasted_iota(jnp.int32, (heads, rows), 0) == slot
    upto = lax.broadcasted_iota(jnp.int32, (rows, rows), 0) <= lax.broadcasted_iota(
        jnp.int32, (rows, rows), 1
    )
    count = dot(hit.astype(BF16), upto.astype(BF16))
    rank = jnp.sum(jnp.where(hit, count, 0.0), 0, keepdims=True).astype(jnp.int32) - 1
    return slot, rank


def half_places(inst, owner_ref, heads, capacity):
    slot, rank = places(inst, owner_ref, heads)
    half = heads // 2
    mine = (slot >= half) == (lax.axis_index("loc") >= half)
    head = jnp.where(slot >= half, slot - half, slot)
    return mine, jnp.where(mine, head, head ^ (half // 2)), rank


def one_hot_back(pos, size):
    column = jnp.transpose(jnp.broadcast_to(pos.astype(F32), (128, pos.shape[1])))[:, :1]
    number = lax.broadcasted_iota(jnp.int32, (pos.shape[1], size), 1)
    return (number == column.astype(jnp.int32)).astype(F32).astype(BF16)


def prep_kernel(heads, capacity, near, inst_ref, owner_ref, x_ref, t_ref, out_ref, place_ref):
    size, width = out_ref.shape[0], x_ref.shape[1]
    step = pl.program_id(0)

    @pl.when(step == 0)
    def _():
        mine, head, rank = half_places(inst_ref[...], owner_ref, heads, capacity)
        place = jnp.where(mine == near, head * capacity + rank, -1)
        place_ref[...] = jnp.broadcast_to(place, place_ref.shape)

    number = lax.broadcasted_iota(jnp.int32, (size, inst_ref.shape[1]), 0) + step * size
    pick = (number == place_ref[0:1, :]).astype(F32).astype(BF16)
    out_ref[:, :width] = dot(pick, x_ref[...]).astype(BF16)
    out_ref[:, width:] = dot(pick, t_ref[...]).astype(BF16)


def back_kernel(heads, capacity, inst_ref, owner_ref, near_ref, far_ref):
    mine, head, rank = half_places(inst_ref[...], owner_ref, heads, capacity)
    place = head * capacity + rank
    near_ref[...] = one_hot_back(jnp.where(mine, place, -1), near_ref.shape[1])
    far_ref[...] = one_hot_back(jnp.where(mine, -1, place), far_ref.shape[1])


def masked(block, pattern_ref, row, column):
    return (block.astype(F32) * pattern_ref[0, row, column].astype(F32)).astype(BF16)


def piece_kernel(w_ref, pattern_ref, weight_ref, *out_refs):
    rows, channels = out_refs[0].shape
    high = weight_ref[...].astype(BF16)
    rest = weight_ref[...] - high.astype(F32)
    middle = rest.astype(BF16)
    low = (rest - middle.astype(F32)).astype(BF16)
    line = lax.broadcasted_iota(jnp.int32, (TERMS, channels), 0)
    terms = jnp.where(line == 0, high.astype(F32), jnp.where(line == 1, middle.astype(F32), 0.0))
    out_refs[-1][rows:, :] = jnp.where(line == 2, low.astype(F32), terms).astype(BF16)
    for chunk, out_ref in enumerate(out_refs):
        first = (lax.axis_index("grp") * len(out_refs) + chunk) * (rows // BLK)
        for i in range(rows // BLK):
            here = pl.ds(pl.multiple_of((first + i) * BLK, BLK), BLK)
            for j in range(channels // BLK):
                cols = slice(j * BLK, (j + 1) * BLK)
                out_ref[i * BLK : (i + 1) * BLK, cols] = masked(
                    w_ref[0, here, cols], pattern_ref, first + i, j
                )


def effective_kernel(w_ref, pattern_ref, out_ref):
    width, channels = out_ref.shape
    for i in range(width // BLK):
        for j in range(channels // BLK):
            rows, cols = slice(i * BLK, (i + 1) * BLK), slice(j * BLK, (j + 1) * BLK)
            out_ref[rows, cols] = masked(w_ref[0, rows, cols], pattern_ref, i, j)


def piece_columns(number, deep):
    first = (lax.axis_index("grp") ^ (number // CHUNKS)) * CHUNKS + number % CHUNKS
    return pl.ds(pl.multiple_of(first * deep, deep), deep)


def far_res_kernel(width, x_ref, *refs):
    eff_refs, res_ref = refs[:-1], refs[-1]
    deep = eff_refs[0].shape[0]
    predicted = dot(x_ref[:, piece_columns(0, deep)], eff_refs[0][:deep])
    for number in range(1, len(eff_refs)):
        predicted += dot(x_ref[:, piece_columns(number, deep)], eff_refs[number][:deep])
    misfit = predicted - x_ref[:, width:].astype(F32)
    terms = eff_refs[CHUNKS - 1][deep:].astype(F32)
    weight = terms[0:1] + terms[1:2] + terms[2:3]
    res_ref[...] = (weight * misfit).astype(BF16)


def far_grad_kernel(res_ref, *refs):
    eff_refs, grad_ref = refs[:-1], refs[-1]
    deep = eff_refs[0].shape[0]
    for number, eff_ref in enumerate(eff_refs):
        grad = dot(res_ref[...], eff_ref[:deep], 1, 1)
        grad_ref[:, piece_columns(number, deep)] = grad.astype(BF16)


def head_kernel(width, x_ref, eff_ref, weight_ref, grad_ref, res_ref):
    predicted = dot(x_ref[:, :width], eff_ref[...])
    residual = (weight_ref[...] * (predicted - x_ref[:, width:].astype(F32))).astype(BF16)
    res_ref[...] = residual
    grad_ref[...] = dot(residual, eff_ref[...], 1, 1).astype(BF16)


def far_raw_kernel(x_ref, res_ref, out_ref):
    out_ref[...] = dot(x_ref[...], res_ref[...], 0, 0).astype(BF16)


def raw_kernel(first, x_ref, res_ref, far_ref, out_ref, pattern_ref, before_ref, raw_ref, square_ref):
    step = pl.program_id(0)
    size, channels = raw_ref.shape
    raw = dot(x_ref[...], res_ref[...], 0, 0) + far_ref[...].astype(F32)
    raw = raw + out_ref[...].astype(F32)

    @pl.when(step == 0)
    def _():
        square_ref[...] = before_ref[...]

    for i in range(size // BLK):
        for j in range(channels // BLK):
            rows, cols = slice(i * BLK, (i + 1) * BLK), slice(j * BLK, (j + 1) * BLK)
            used = pattern_ref[0, first + step * (size // BLK) + i, j].astype(F32)
            part = raw[rows, cols] * used
            raw_ref[rows, cols] = part
            square_ref[...] += jnp.sum((part * part).reshape(BLK // 8, 8, BLK), 0)


def far_place_kernel(back_ref, got_ref, out_ref):
    out_ref[...] = dot(back_ref[...], got_ref[...]).astype(BF16)


def finish_kernel(limit, parts, back_ref, got_ref, far_ref, square_ref, *refs):
    raw_refs, (out_ref, head_ref) = refs[:parts], refs[parts:]
    squares = jnp.sum(square_ref[...], keepdims=True)
    factor = jnp.minimum(1.0, limit / jnp.sqrt(squares + 1e-06))
    step = pl.program_id(0)
    per = pl.num_programs(0) // parts
    for part in range(parts):

        @pl.when(step // per == part)
        def _():
            head_ref[...] = (raw_refs[part][...] * factor)[None]

    out = dot(back_ref[...], got_ref[...]) + far_ref[...].astype(F32)
    out_ref[...] = out.astype(BF16)


def per_device(latents, obs_inst, owner_slot, head_weights, error_weight, block_pattern, targets):
    members, groups = lax.axis_size("loc"), lax.axis_size("grp")
    local_heads, width, channels = head_weights.shape
    heads = local_heads * members
    rows = latents.shape[0]
    capacity = 2 * rows // heads
    half = members // 2
    placed = half * capacity
    apart = half + half // 2
    wide = width + channels
    inst = obs_inst.reshape(1, rows)
    halves = [list(range(half)), list(range(half, members))]

    def partner(x):
        return lax.ppermute(x, "loc", [(i, i ^ apart) for i in range(members)])

    def hop(x, distance):
        return lax.ppermute(x, "loc", [(i, i ^ distance) for i in range(members)])

    def in_half(x):
        return lax.all_to_all(
            x, "loc", split_axis=0, concat_axis=0, tiled=True, axis_index_groups=halves
        )

    cut = 4

    def prep(near, name):
        return pl.pallas_call(
            functools.partial(prep_kernel, heads, capacity, near),
            grid=(2,),
            in_specs=[whole((1, rows)), SMEM, whole((rows, width)), whole((rows, channels))],
            out_specs=pl.BlockSpec((placed // 2, wide), lambda i: (i, 0)),
            out_shape=jax.ShapeDtypeStruct((placed, wide), BF16),
            scratch_shapes=[pltpu.VMEM((8, rows), jnp.int32)],
            compiler_params=STREAM,
            cost_estimate=cost(2 * placed * rows * wide, 2 * (placed + rows) * wide),
            name=name,
        )(inst, owner_slot, latents, targets)

    far_send = prep(False, "prep_far")
    near_send = prep(True, "prep_near")
    deep = width // (groups * CHUNKS)
    head_weights, far_send = lax.optimization_barrier((head_weights, far_send))
    pieces = pl.pallas_call(
        piece_kernel,
        in_specs=[VMEM, SMEM, VMEM],
        out_specs=[VMEM] * CHUNKS,
        out_shape=[
            jax.ShapeDtypeStruct((deep + (TERMS if last else 0), channels), BF16)
            for last in [False] * (CHUNKS - 1) + [True]
        ],
        compiler_params=STREAM,
        cost_estimate=cost(CHUNKS * deep * channels, 4 * CHUNKS * deep * channels),
        name="piece",
    )(head_weights, block_pattern, error_weight)
    crossed = [partner(piece) for piece in pieces]
    crossed[0], near_send = lax.optimization_barrier((crossed[0], near_send))
    swapped = [[piece] for piece in crossed]
    step = 1
    while step < groups:
        swap = [(i, i ^ step) for i in range(groups)]
        swapped = [held + [lax.ppermute(x, "grp", swap) for x in held] for held in swapped]
        step *= 2
    far_x = in_half(far_send)
    early = swapped[: CHUNKS // 4]
    near_send, far_x, early, crossed = lax.optimization_barrier((near_send, far_x, early, crossed))
    swapped[: CHUNKS // 4] = early
    far_eff = [swapped[chunk][number] for number in range(groups) for chunk in range(CHUNKS)]
    near_x = in_half(near_send)

    near_back, far_back = pl.pallas_call(
        functools.partial(back_kernel, heads, capacity),
        in_specs=[VMEM, SMEM],
        out_specs=[VMEM, VMEM],
        out_shape=[jax.ShapeDtypeStruct((rows, placed), BF16)] * 2,
        compiler_params=SMALL,
        cost_estimate=cost(2 * rows * rows * 128, 4 * rows * placed),
        name="back_places",
    )(inst, owner_slot)
    effective = pl.pallas_call(
        effective_kernel,
        in_specs=[VMEM, SMEM],
        out_specs=VMEM,
        out_shape=jax.ShapeDtypeStruct((width, channels), BF16),
        compiler_params=SMALL,
        cost_estimate=cost(width * channels, 4 * width * channels),
        name="effective",
    )(head_weights, block_pattern)
    far_x, effective, near_back, far_back = lax.optimization_barrier(
        (far_x, effective, near_back, far_back)
    )

    size = placed // 2
    row_spec = pl.BlockSpec((size, wide), lambda i: (i, 0))
    res_spec = pl.BlockSpec((size, channels), lambda i: (i, 0))
    far_specs = [whole(piece.shape) for piece in far_eff]
    far_res = pl.pallas_call(
        functools.partial(far_res_kernel, width),
        grid=(2,),
        in_specs=[row_spec] + far_specs,
        out_specs=res_spec,
        out_shape=jax.ShapeDtypeStruct((placed, channels), BF16),
        compiler_params=SMALL,
        cost_estimate=cost(2 * placed * width * channels, 2 * placed * wide),
        name="far_res",
    )(far_x, *far_eff)

    tall = 512
    steps = width // (PARTS * tall)
    far_raw = []
    for chunk in range(PARTS):
        part = pl.pallas_call(
            far_raw_kernel,
            grid=(steps,),
            in_specs=[
                pl.BlockSpec((placed, tall), lambda i, chunk=chunk: (0, chunk * steps + i)),
                whole((placed, channels)),
            ],
            out_specs=pl.BlockSpec((tall, channels), lambda i: (i, 0)),
            out_shape=jax.ShapeDtypeStruct((width // PARTS, channels), BF16),
            compiler_params=SMALL,
            cost_estimate=cost(2 * placed * width * channels // PARTS, 2 * width * channels),
            name="far_raw",
        )(far_x, far_res)
        far_raw.append(part)
    sent = far_raw
    bit = half // 2
    inner = [i for i in range(members) if (i // bit) % 2 != (i // half) % 2]
    outer = [i for i in range(members) if i not in inner]
    far_raw = [lax.ppermute(part, "loc", [(i, i ^ apart) for i in inner]) for part in sent]
    near_x, held = lax.optimization_barrier((near_x, sent))
    far_out = [lax.ppermute(part, "loc", [(i, i ^ apart) for i in outer]) for part in held]

    grad_spec = pl.BlockSpec((size, width), lambda i: (i, 0))
    far_grad = pl.pallas_call(
        far_grad_kernel,
        grid=(2,),
        in_specs=[res_spec] + far_specs,
        out_specs=grad_spec,
        out_shape=jax.ShapeDtypeStruct((placed, width), BF16),
        compiler_params=SMALL,
        cost_estimate=cost(2 * placed * width * channels, 2 * placed * wide),
        name="far_grad",
    )(far_res, *far_eff)
    far_grad, sent = lax.optimization_barrier((far_grad, sent))
    far_got = in_half(far_grad)
    near_grad, near_res = pl.pallas_call(
        functools.partial(head_kernel, width),
        grid=(2,),
        in_specs=[row_spec, whole((width, channels)), whole((1, channels))],
        out_specs=[grad_spec, res_spec],
        out_shape=[
            jax.ShapeDtypeStruct((placed, width), BF16),
            jax.ShapeDtypeStruct((placed, channels), BF16),
        ],
        compiler_params=SMALL,
        cost_estimate=LATE,
        name="near_head",
    )(near_x, effective, error_weight)
    near_grad, far_got = lax.optimization_barrier((near_grad, far_got))

    def column_spec(deep):
        return pl.BlockSpec((deep, width // cut), lambda i: (0, i))

    def half_spec(deep):
        return pl.BlockSpec((deep, width // 2), lambda i: (0, i))

    far_placed = pl.pallas_call(
        far_place_kernel,
        grid=(2,),
        in_specs=[whole((rows, placed)), half_spec(placed)],
        out_specs=half_spec(rows),
        out_shape=jax.ShapeDtypeStruct((rows, width), BF16),
        compiler_params=STREAM,
        cost_estimate=cost(2 * rows * placed * width, 4 * placed * width),
        name="far_place",
    )(far_back, far_got)
    near_grad, far_placed = lax.optimization_barrier((near_grad, far_placed))
    near_got = in_half(near_grad)
    raw_grad, squares = [], jnp.zeros((8, 128), F32)
    for chunk in range(PARTS):
        part, squares = pl.pallas_call(
            functools.partial(raw_kernel, chunk * steps * (tall // BLK)),
            grid=(steps,),
            in_specs=[
                pl.BlockSpec((placed, tall), lambda i, chunk=chunk: (0, chunk * steps + i)),
                whole((placed, channels)),
                pl.BlockSpec((tall, channels), lambda i: (i, 0)),
                pl.BlockSpec((tall, channels), lambda i: (i, 0)),
                SMEM,
                whole((8, 128)),
            ],
            out_specs=[pl.BlockSpec((tall, channels), lambda i: (i, 0)), whole((8, 128))],
            out_shape=[
                jax.ShapeDtypeStruct((width // PARTS, channels), F32),
                jax.ShapeDtypeStruct((8, 128), F32),
            ],
            compiler_params=SMALL,
            cost_estimate=LATE,
            name="raw",
        )(near_x, near_res, far_raw[chunk], far_out[chunk], block_pattern, squares)
        raw_grad.append(part)
    step = 1
    while step < members:
        ways = min(4, members // step)
        squares = squares + sum(hop(squares, step * way) for way in range(1, ways))
        step *= ways

    cut = 2
    near_got, squares = lax.optimization_barrier((near_got, squares))

    def raw_spec(part):
        low = part * (cut // PARTS)
        return pl.BlockSpec(
            (width // cut, channels), lambda i: (jnp.clip(i - low, 0, cut // PARTS - 1), 0)
        )

    latent_grad, head_grad = pl.pallas_call(
        functools.partial(finish_kernel, math.sqrt(heads * width * channels), PARTS),
        grid=(cut,),
        in_specs=[whole((rows, placed)), column_spec(placed), column_spec(rows), whole((8, 128))]
        + [raw_spec(part) for part in range(PARTS)],
        out_specs=[
            column_spec(rows),
            pl.BlockSpec((1, width // cut, channels), lambda i: (0, i, 0)),
        ],
        out_shape=[
            jax.ShapeDtypeStruct((rows, width), BF16),
            jax.ShapeDtypeStruct((1, width, channels), F32),
        ],
        compiler_params=STREAM,
        cost_estimate=cost(2 * rows * placed * width, 8 * width * channels),
        name="finish",
    )(near_back, near_got, far_placed, squares, *raw_grad)
    return (latent_grad, head_grad)


def solution(mesh):
    in_specs = (
        P(("grp", "loc"), None),
        P(("grp", "loc"), None),
        P(),
        P("loc", None, None),
        P("loc", None),
        P("loc", None, None),
        P(("grp", "loc"), None),
    )
    out_specs = (P(("grp", "loc"), None), P(("grp", "loc"), None, None))
    return jax.shard_map(
        per_device, mesh=mesh, in_specs=in_specs, out_specs=out_specs, check_vma=False
    )
```

```python
import functools
import math

import jax
import jax.numpy as jnp
from jax import lax
from jax.experimental import pallas as pl
from jax.experimental.pallas import tpu as pltpu
from jax.sharding import PartitionSpec as P


BLK = 128
TERMS = 16
CHUNKS = 4
PARTS = 2
F32 = jnp.float32
BF16 = jnp.bfloat16
VMEM = pl.BlockSpec(memory_space=pltpu.VMEM)
SMEM = pl.BlockSpec(memory_space=pltpu.SMEM)
STREAM = pltpu.CompilerParams(vmem_limit_bytes=60 * 1024 * 1024)
SMALL = pltpu.CompilerParams(vmem_limit_bytes=24 * 1024 * 1024)


def dot(a, b, ca=1, cb=0):
    return lax.dot_general(a, b, (((ca,), (cb,)), ((), ())), preferred_element_type=F32)


def cost(flops, nbytes):
    return pl.CostEstimate(flops=int(flops), bytes_accessed=int(nbytes), transcendentals=0)


LATE = cost(1 << 40, 1 << 30)


def whole(shape):
    return pl.BlockSpec(shape, lambda i: (0,) * len(shape))


def places(inst, owner_ref, heads):
    rows = inst.shape[1]
    slot = jnp.zeros_like(inst)
    for k in range(heads):
        slot = jnp.where(inst == k, owner_ref[k], slot)
    hit = lax.broadcasted_iota(jnp.int32, (heads, rows), 0) == slot
    upto = lax.broadcasted_iota(jnp.int32, (rows, rows), 0) <= lax.broadcasted_iota(
        jnp.int32, (rows, rows), 1
    )
    count = dot(hit.astype(BF16), upto.astype(BF16))
    rank = jnp.sum(jnp.where(hit, count, 0.0), 0, keepdims=True).astype(jnp.int32) - 1
    return slot, rank


def half_places(inst, owner_ref, heads, capacity):
    slot, rank = places(inst, owner_ref, heads)
    half = heads // 2
    mine = (slot >= half) == (lax.axis_index("loc") >= half)
    head = jnp.where(slot >= half, slot - half, slot)
    return mine, jnp.where(mine, head, head ^ (half // 2)), rank


def one_hot_back(pos, size):
    column = jnp.transpose(jnp.broadcast_to(pos.astype(F32), (128, pos.shape[1])))[:, :1]
    number = lax.broadcasted_iota(jnp.int32, (pos.shape[1], size), 1)
    return (number == column.astype(jnp.int32)).astype(F32).astype(BF16)


def prep_kernel(heads, capacity, near, inst_ref, owner_ref, x_ref, t_ref, out_ref, place_ref):
    size, width = out_ref.shape[0], x_ref.shape[1]
    step = pl.program_id(0)

    @pl.when(step == 0)
    def _():
        mine, head, rank = half_places(inst_ref[...], owner_ref, heads, capacity)
        place = jnp.where(mine == near, head * capacity + rank, -1)
        place_ref[...] = jnp.broadcast_to(place, place_ref.shape)

    number = lax.broadcasted_iota(jnp.int32, (size, inst_ref.shape[1]), 0) + step * size
    pick = (number == place_ref[0:1, :]).astype(F32).astype(BF16)
    out_ref[:, :width] = dot(pick, x_ref[...]).astype(BF16)
    out_ref[:, width:] = dot(pick, t_ref[...]).astype(BF16)


def back_kernel(heads, capacity, inst_ref, owner_ref, near_ref, far_ref):
    mine, head, rank = half_places(inst_ref[...], owner_ref, heads, capacity)
    place = head * capacity + rank
    near_ref[...] = one_hot_back(jnp.where(mine, place, -1), near_ref.shape[1])
    far_ref[...] = one_hot_back(jnp.where(mine, -1, place), far_ref.shape[1])


def masked(block, pattern_ref, row, column):
    return (block.astype(F32) * pattern_ref[0, row, column].astype(F32)).astype(BF16)


def piece_kernel(w_ref, pattern_ref, weight_ref, *out_refs):
    rows, channels = out_refs[0].shape
    high = weight_ref[...].astype(BF16)
    rest = weight_ref[...] - high.astype(F32)
    middle = rest.astype(BF16)
    low = (rest - middle.astype(F32)).astype(BF16)
    line = lax.broadcasted_iota(jnp.int32, (TERMS, channels), 0)
    terms = jnp.where(line == 0, high.astype(F32), jnp.where(line == 1, middle.astype(F32), 0.0))
    out_refs[-1][rows:, :] = jnp.where(line == 2, low.astype(F32), terms).astype(BF16)
    for chunk, out_ref in enumerate(out_refs):
        first = (lax.axis_index("grp") * len(out_refs) + chunk) * (rows // BLK)
        for i in range(rows // BLK):
            here = pl.ds(pl.multiple_of((first + i) * BLK, BLK), BLK)
            for j in range(channels // BLK):
                cols = slice(j * BLK, (j + 1) * BLK)
                out_ref[i * BLK : (i + 1) * BLK, cols] = masked(
                    w_ref[0, here, cols], pattern_ref, first + i, j
                )


def effective_kernel(w_ref, pattern_ref, out_ref):
    width, channels = out_ref.shape
    for i in range(width // BLK):
        for j in range(channels // BLK):
            rows, cols = slice(i * BLK, (i + 1) * BLK), slice(j * BLK, (j + 1) * BLK)
            out_ref[rows, cols] = masked(w_ref[0, rows, cols], pattern_ref, i, j)


def piece_columns(number, deep):
    first = (lax.axis_index("grp") ^ (number // CHUNKS)) * CHUNKS + number % CHUNKS
    return pl.ds(pl.multiple_of(first * deep, deep), deep)


def far_res_kernel(width, x_ref, *refs):
    eff_refs, res_ref = refs[:-1], refs[-1]
    deep = eff_refs[0].shape[0]
    predicted = dot(x_ref[:, piece_columns(0, deep)], eff_refs[0][:deep])
    for number in range(1, len(eff_refs)):
        predicted += dot(x_ref[:, piece_columns(number, deep)], eff_refs[number][:deep])
    misfit = predicted - x_ref[:, width:].astype(F32)
    terms = eff_refs[CHUNKS - 1][deep:].astype(F32)
    weight = terms[0:1] + terms[1:2] + terms[2:3]
    res_ref[...] = (weight * misfit).astype(BF16)


def far_grad_kernel(res_ref, *refs):
    eff_refs, grad_ref = refs[:-1], refs[-1]
    deep = eff_refs[0].shape[0]
    for number, eff_ref in enumerate(eff_refs):
        grad = dot(res_ref[...], eff_ref[:deep], 1, 1)
        grad_ref[:, piece_columns(number, deep)] = grad.astype(BF16)


def head_kernel(width, x_ref, eff_ref, weight_ref, grad_ref, res_ref):
    predicted = dot(x_ref[:, :width], eff_ref[...])
    residual = (weight_ref[...] * (predicted - x_ref[:, width:].astype(F32))).astype(BF16)
    res_ref[...] = residual
    grad_ref[...] = dot(residual, eff_ref[...], 1, 1).astype(BF16)


def far_raw_kernel(x_ref, res_ref, out_ref):
    out_ref[...] = dot(x_ref[...], res_ref[...], 0, 0).astype(BF16)


def raw_kernel(first, x_ref, res_ref, far_ref, out_ref, pattern_ref, before_ref, raw_ref, square_ref):
    step = pl.program_id(0)
    size, channels = raw_ref.shape
    raw = dot(x_ref[...], res_ref[...], 0, 0) + far_ref[...].astype(F32)
    raw = raw + out_ref[...].astype(F32)

    @pl.when(step == 0)
    def _():
        square_ref[...] = before_ref[...]

    for i in range(size // BLK):
        for j in range(channels // BLK):
            rows, cols = slice(i * BLK, (i + 1) * BLK), slice(j * BLK, (j + 1) * BLK)
            used = pattern_ref[0, first + step * (size // BLK) + i, j].astype(F32)
            part = raw[rows, cols] * used
            raw_ref[rows, cols] = part
            square_ref[...] += jnp.sum((part * part).reshape(BLK // 8, 8, BLK), 0)


def far_place_kernel(back_ref, got_ref, out_ref):
    out_ref[...] = dot(back_ref[...], got_ref[...]).astype(BF16)


def finish_kernel(limit, parts, back_ref, got_ref, far_ref, square_ref, *refs):
    raw_refs, (out_ref, head_ref) = refs[:parts], refs[parts:]
    squares = jnp.sum(square_ref[...], keepdims=True)
    factor = jnp.minimum(1.0, limit / jnp.sqrt(squares + 1e-06))
    step = pl.program_id(0)
    per = pl.num_programs(0) // parts
    for part in range(parts):

        @pl.when(step // per == part)
        def _():
            head_ref[...] = (raw_refs[part][...] * factor)[None]

    out = dot(back_ref[...], got_ref[...]) + far_ref[...].astype(F32)
    out_ref[...] = out.astype(BF16)


def per_device(latents, obs_inst, owner_slot, head_weights, error_weight, block_pattern, targets):
    members, groups = lax.axis_size("loc"), lax.axis_size("grp")
    local_heads, width, channels = head_weights.shape
    heads = local_heads * members
    rows = latents.shape[0]
    capacity = 2 * rows // heads
    half = members // 2
    placed = half * capacity
    apart = half + half // 2
    wide = width + channels
    inst = obs_inst.reshape(1, rows)
    halves = [list(range(half)), list(range(half, members))]

    def partner(x):
        return lax.ppermute(x, "loc", [(i, i ^ apart) for i in range(members)])

    def hop(x, distance):
        return lax.ppermute(x, "loc", [(i, i ^ distance) for i in range(members)])

    def in_half(x):
        return lax.all_to_all(
            x, "loc", split_axis=0, concat_axis=0, tiled=True, axis_index_groups=halves
        )

    cut = 4

    def prep(near, name):
        return pl.pallas_call(
            functools.partial(prep_kernel, heads, capacity, near),
            grid=(2,),
            in_specs=[whole((1, rows)), SMEM, whole((rows, width)), whole((rows, channels))],
            out_specs=pl.BlockSpec((placed // 2, wide), lambda i: (i, 0)),
            out_shape=jax.ShapeDtypeStruct((placed, wide), BF16),
            scratch_shapes=[pltpu.VMEM((8, rows), jnp.int32)],
            compiler_params=STREAM,
            cost_estimate=cost(2 * placed * rows * wide, 2 * (placed + rows) * wide),
            name=name,
        )(inst, owner_slot, latents, targets)

    far_send = prep(False, "prep_far")
    near_send = prep(True, "prep_near")
    deep = width // (groups * CHUNKS)
    head_weights, far_send = lax.optimization_barrier((head_weights, far_send))
    pieces = pl.pallas_call(
        piece_kernel,
        in_specs=[VMEM, SMEM, VMEM],
        out_specs=[VMEM] * CHUNKS,
        out_shape=[
            jax.ShapeDtypeStruct((deep + (TERMS if last else 0), channels), BF16)
            for last in [False] * (CHUNKS - 1) + [True]
        ],
        compiler_params=STREAM,
        cost_estimate=cost(CHUNKS * deep * channels, 4 * CHUNKS * deep * channels),
        name="piece",
    )(head_weights, block_pattern, error_weight)
    crossed = [partner(piece) for piece in pieces]
    crossed[0], near_send = lax.optimization_barrier((crossed[0], near_send))
    swapped = [[piece] for piece in crossed]
    step = 1
    while step < groups:
        swap = [(i, i ^ step) for i in range(groups)]
        swapped = [held + [lax.ppermute(x, "grp", swap) for x in held] for held in swapped]
        step *= 2
    far_x = in_half(far_send)
    early = swapped[: CHUNKS // 4]
    near_send, far_x, early, crossed = lax.optimization_barrier((near_send, far_x, early, crossed))
    swapped[: CHUNKS // 4] = early
    far_eff = [swapped[chunk][number] for number in range(groups) for chunk in range(CHUNKS)]
    near_x = in_half(near_send)

    near_back, far_back = pl.pallas_call(
        functools.partial(back_kernel, heads, capacity),
        in_specs=[VMEM, SMEM],
        out_specs=[VMEM, VMEM],
        out_shape=[jax.ShapeDtypeStruct((rows, placed), BF16)] * 2,
        compiler_params=SMALL,
        cost_estimate=LATE,
        name="back_places",
    )(inst, owner_slot)
    effective = pl.pallas_call(
        effective_kernel,
        in_specs=[VMEM, SMEM],
        out_specs=VMEM,
        out_shape=jax.ShapeDtypeStruct((width, channels), BF16),
        compiler_params=SMALL,
        cost_estimate=LATE,
        name="effective",
    )(head_weights, block_pattern)
    far_x, effective, near_back, far_back = lax.optimization_barrier(
        (far_x, effective, near_back, far_back)
    )

    size = placed // 2
    row_spec = pl.BlockSpec((size, wide), lambda i: (i, 0))
    res_spec = pl.BlockSpec((size, channels), lambda i: (i, 0))
    far_specs = [whole(piece.shape) for piece in far_eff]
    far_res = pl.pallas_call(
        functools.partial(far_res_kernel, width),
        grid=(2,),
        in_specs=[row_spec] + far_specs,
        out_specs=res_spec,
        out_shape=jax.ShapeDtypeStruct((placed, channels), BF16),
        compiler_params=SMALL,
        cost_estimate=cost(2 * placed * width * channels, 2 * placed * wide),
        name="far_res",
    )(far_x, *far_eff)

    tall = 512
    steps = width // (PARTS * tall)
    far_raw = []
    for chunk in range(PARTS):
        part = pl.pallas_call(
            far_raw_kernel,
            grid=(steps,),
            in_specs=[
                pl.BlockSpec((placed, tall), lambda i, chunk=chunk: (0, chunk * steps + i)),
                whole((placed, channels)),
            ],
            out_specs=pl.BlockSpec((tall, channels), lambda i: (i, 0)),
            out_shape=jax.ShapeDtypeStruct((width // PARTS, channels), BF16),
            compiler_params=SMALL,
            cost_estimate=cost(2 * placed * width * channels // PARTS, 2 * width * channels),
            name="far_raw",
        )(far_x, far_res)
        far_raw.append(part)
    sent = far_raw
    bit = half // 2
    inner = [i for i in range(members) if (i // bit) % 2 != (i // half) % 2]
    outer = [i for i in range(members) if i not in inner]
    far_raw = [lax.ppermute(part, "loc", [(i, i ^ apart) for i in inner]) for part in sent]
    near_x, held = lax.optimization_barrier((near_x, sent))
    far_out = [lax.ppermute(part, "loc", [(i, i ^ apart) for i in outer]) for part in held]

    grad_spec = pl.BlockSpec((size, width), lambda i: (i, 0))
    far_grad = pl.pallas_call(
        far_grad_kernel,
        grid=(2,),
        in_specs=[res_spec] + far_specs,
        out_specs=grad_spec,
        out_shape=jax.ShapeDtypeStruct((placed, width), BF16),
        compiler_params=SMALL,
        cost_estimate=cost(2 * placed * width * channels, 2 * placed * wide),
        name="far_grad",
    )(far_res, *far_eff)
    far_grad, sent = lax.optimization_barrier((far_grad, sent))
    far_got = in_half(far_grad)
    near_grad, near_res = pl.pallas_call(
        functools.partial(head_kernel, width),
        grid=(2,),
        in_specs=[row_spec, whole((width, channels)), whole((1, channels))],
        out_specs=[grad_spec, res_spec],
        out_shape=[
            jax.ShapeDtypeStruct((placed, width), BF16),
            jax.ShapeDtypeStruct((placed, channels), BF16),
        ],
        compiler_params=SMALL,
        cost_estimate=LATE,
        name="near_head",
    )(near_x, effective, error_weight)
    near_grad, far_got = lax.optimization_barrier((near_grad, far_got))

    def column_spec(deep):
        return pl.BlockSpec((deep, width // cut), lambda i: (0, i))

    def half_spec(deep):
        return pl.BlockSpec((deep, width // 2), lambda i: (0, i))

    far_placed = pl.pallas_call(
        far_place_kernel,
        grid=(2,),
        in_specs=[whole((rows, placed)), half_spec(placed)],
        out_specs=half_spec(rows),
        out_shape=jax.ShapeDtypeStruct((rows, width), BF16),
        compiler_params=STREAM,
        cost_estimate=cost(2 * rows * placed * width, 4 * placed * width),
        name="far_place",
    )(far_back, far_got)
    near_grad, far_placed = lax.optimization_barrier((near_grad, far_placed))
    near_got = in_half(near_grad)
    raw_grad, squares = [], jnp.zeros((8, 128), F32)
    for chunk in range(PARTS):
        part, squares = pl.pallas_call(
            functools.partial(raw_kernel, chunk * steps * (tall // BLK)),
            grid=(steps,),
            in_specs=[
                pl.BlockSpec((placed, tall), lambda i, chunk=chunk: (0, chunk * steps + i)),
                whole((placed, channels)),
                pl.BlockSpec((tall, channels), lambda i: (i, 0)),
                pl.BlockSpec((tall, channels), lambda i: (i, 0)),
                SMEM,
                whole((8, 128)),
            ],
            out_specs=[pl.BlockSpec((tall, channels), lambda i: (i, 0)), whole((8, 128))],
            out_shape=[
                jax.ShapeDtypeStruct((width // PARTS, channels), F32),
                jax.ShapeDtypeStruct((8, 128), F32),
            ],
            compiler_params=SMALL,
            cost_estimate=LATE,
            name="raw",
        )(near_x, near_res, far_raw[chunk], far_out[chunk], block_pattern, squares)
        raw_grad.append(part)
    step = 1
    while step < members:
        ways = min(4, members // step)
        squares = squares + sum(hop(squares, step * way) for way in range(1, ways))
        step *= ways

    cut = 2
    near_got, squares = lax.optimization_barrier((near_got, squares))

    def raw_spec(part):
        low = part * (cut // PARTS)
        return pl.BlockSpec(
            (width // cut, channels), lambda i: (jnp.clip(i - low, 0, cut // PARTS - 1), 0)
        )

    latent_grad, head_grad = pl.pallas_call(
        functools.partial(finish_kernel, math.sqrt(heads * width * channels), PARTS),
        grid=(cut,),
        in_specs=[whole((rows, placed)), column_spec(placed), column_spec(rows), whole((8, 128))]
        + [raw_spec(part) for part in range(PARTS)],
        out_specs=[
            column_spec(rows),
            pl.BlockSpec((1, width // cut, channels), lambda i: (0, i, 0)),
        ],
        out_shape=[
            jax.ShapeDtypeStruct((rows, width), BF16),
            jax.ShapeDtypeStruct((1, width, channels), F32),
        ],
        compiler_params=STREAM,
        cost_estimate=cost(2 * rows * placed * width, 8 * width * channels),
        name="finish",
    )(near_back, near_got, far_placed, squares, *raw_grad)
    return (latent_grad, head_grad)


def solution(mesh):
    in_specs = (
        P(("grp", "loc"), None),
        P(("grp", "loc"), None),
        P(),
        P("loc", None, None),
        P("loc", None),
        P("loc", None, None),
        P(("grp", "loc"), None),
    )
    out_specs = (P(("grp", "loc"), None), P(("grp", "loc"), None, None))
    return jax.shard_map(
        per_device, mesh=mesh, in_specs=in_specs, out_specs=out_specs, check_vma=False
    )
```
